256 devices in a mesh: blk: 64 (over z, y_lo, x), col: 4 (over y_hi, core).
Axes of the slice: x: 4, y: 4 (y_hi: 2, y_lo: 2; y = y_hi * 2 + y_lo), z: 8, core: 2. Of those that a mesh axis runs over, the one named last changes fastest.
Arguments:
- slab: float32 [131072, 1024], P('blk', 'col'), may hold values from -6 to 6
- angles: float32 [4, 65536], P(None, 'blk'), may hold values from -3.140625 to 3.140625
- pairing: int32 [4], replicated, may hold values from 0 to 1, as said below
- band_offsets: int32 [8], replicated, may hold values from 1 to 512, as said below
- band_weights: float32 [8], replicated, may hold values from -0.0625 to 0.0625
Outputs:
- evolved: float32 [131072, 1024], P('blk', 'col')
- angle_gradient: float32 [4, 65536], P(None, 'blk')
The draws below stay inside these ranges and needn't reach their ends.
Inputs may be any that keep to these rules, and one draw needn't show every extreme that they name: `pairing`: the entries alternate between 0 and 1 from one layer to the next. `band_offsets`: exactly one entry equals 512.
All inputs are finite; a program needn't handle non-finite values.
Results may differ from the reference program's by a relative error of at most 0.0001.
Values sent between devices are 32-bit elements; how exact they have to be, the bound alone decides.
No kernel may reach another device: no remote copies, remote signals or barrier semaphores. Data moves between devices by JAX's collectives and lax.ppermute only.
A program may use at most 128 MiB of HBM per device.

```python
import jax
import jax.numpy as jnp

LAYERS = 4
REACH = 512
BANDS = 8
ROWS = 131072
PAIRS = 65536
SLAB_COLS = 1024


def draw_pairing(key, part):
    leading = jax.random.randint(jax.random.fold_in(key, 7), (), 0, 2)
    steps = jnp.arange(LAYERS, dtype=jnp.int32)
    return ((steps + leading) % 2).astype(jnp.int32)


def draw_band_offsets(key, part):
    values = jax.random.randint(jax.random.fold_in(key, 11), (BANDS,), 1, REACH)
    where = jax.random.randint(jax.random.fold_in(key, 13), (), 0, BANDS)
    slots = jnp.arange(BANDS, dtype=jnp.int32)
    return jnp.where(slots == where, REACH, values).astype(jnp.int32)


def steps_of(stream_key, extent, shards, least, high):
    def one(dim, blocks):
        steps = jax.random.uniform(jax.random.fold_in(jax.random.fold_in(stream_key, 6), dim), (blocks,), jnp.float32, least / len(shards), high / len(shards))
        return jnp.repeat(jnp.exp(steps), extent[dim] // blocks).reshape((-1,) + (1,) * (len(extent) - dim - 1))

    factor_of = one(*shards[0])
    for cut in shards[1:]:
        factor_of = factor_of * one(*cut)
    return factor_of


def normal_values(key, extent, deviation, most, pieces=(), kind=jnp.bfloat16):
    level = steps_of(key, extent, pieces, -0.22, 0.18) if pieces else 1.0
    values = jax.random.normal(key, extent, jnp.float32) * deviation * level
    return jnp.minimum(jnp.maximum(values, -most), most).astype(kind)


def setup_inputs(seed: int = 0) -> dict:
    splits = jax.random.split(jax.random.key(seed), 6)
    slab = normal_values(splits[0], (ROWS, SLAB_COLS), 1.0, 6.0, ((0, 64), (1, 4)), jnp.float32)
    angles = jnp.clip(jax.random.uniform(splits[1], (LAYERS, PAIRS), jnp.float32, -3.140625, 3.140625), -3.140625, 3.140625)
    pairing = draw_pairing(jax.random.fold_in(splits[5], 71), 0)
    band_offsets = draw_band_offsets(jax.random.fold_in(splits[5], 71), 0)
    band_weights = normal_values(splits[4], (BANDS,), (BANDS * SLAB_COLS) ** -0.5, 0.0625, (), jnp.float32)
    return dict(slab=slab, angles=angles, pairing=pairing, band_offsets=band_offsets, band_weights=band_weights)


def rotate(field, offset, cosine, sine):
    rolled = jnp.roll(field, -offset, 0).reshape(field.shape[0] // 2, 2, field.shape[1])
    first = rolled[:, 0]
    second = rolled[:, 1]
    new_first = cosine[:, None] * first - sine[:, None] * second
    new_second = sine[:, None] * first + cosine[:, None] * second
    flat = jnp.stack([new_first, new_second], 1).reshape(field.shape)
    return jnp.roll(flat, offset, 0)


def reference(slab, angles, pairing, band_offsets, band_weights):
    state = slab
    after = []
    for layer in range(LAYERS):
        state = rotate(state, pairing[layer], jnp.cos(angles[layer]), jnp.sin(angles[layer]))
        after.append(state)
    adjoint = jnp.zeros_like(state)
    for band in range(BANDS):
        shift = band_offsets[band]
        adjoint = adjoint + band_weights[band] * (jnp.roll(state, -shift, 0) + jnp.roll(state, shift, 0))
    grads = [None] * LAYERS
    for layer in reversed(range(LAYERS)):
        offset = pairing[layer]
        rolled_state = jnp.roll(after[layer], -offset, 0).reshape(ROWS // 2, 2, SLAB_COLS)
        rolled_adj = jnp.roll(adjoint, -offset, 0).reshape(ROWS // 2, 2, SLAB_COLS)
        grads[layer] = jnp.sum(rolled_adj[:, 1] * rolled_state[:, 0] - rolled_adj[:, 0] * rolled_state[:, 1], axis=1)
        adjoint = rotate(adjoint, offset, jnp.cos(angles[layer]), -jnp.sin(angles[layer]))
    return state, jnp.stack(grads)
```

```python
import jax
import jax.numpy as jnp
from jax import lax
from jax.experimental import pallas as pl
from jax.experimental.pallas import tpu as pltpu
from jax.sharding import PartitionSpec as P

LAYERS = 4
REACH = 512
BANDS = 8
ROWS = 2048
PAIRS = 1024
HALO = 520
STEP = 32
FRONT = 8
GFRONT = 112
INNER = 1024
EDGE = 800


def turn_table(cos_sin, table, tile_of, tiles):
    for tile in range(tiles):
        angle = tile_of(tile)
        both = jnp.concatenate([jnp.cos(angle), jnp.sin(angle)], 0)
        tall = jnp.transpose(both)
        for lane in range(2 * LAYERS):
            cos_sin[table, lane, pl.ds(128 * tile, 128), :] = jnp.broadcast_to(tall[:, lane : lane + 1], (128, 128))


def forward(raw, states, cos_sin, table, shift, lead, pairs):
    for layer in range(LAYERS):
        odd = layer % 2

        def block(i, carry, layer=layer, odd=odd):
            at = pl.multiple_of(i * STEP, STEP)
            angle_at = at + shift + lead if odd else at + shift
            cosine = cos_sin[table, layer, pl.ds(angle_at, STEP), :]
            sine = cos_sin[table, LAYERS + layer, pl.ds(angle_at, STEP), :]
            for half in range(2):
                if layer == 0:
                    first = raw[half, pl.ds(2 * at + lead, STEP, stride=2), :]
                    second = raw[half, pl.ds(2 * at + lead + 1, STEP, stride=2), :]
                elif odd:
                    first = states[layer - 1, 1, half, pl.ds(at + FRONT, STEP), :]
                    second = states[layer - 1, 0, half, pl.ds(at + FRONT + 1, STEP), :]
                else:
                    first = states[layer - 1, 0, half, pl.ds(at + FRONT - 1, STEP), :]
                    second = states[layer - 1, 1, half, pl.ds(at + FRONT, STEP), :]
                new_first = cosine * first - sine * second
                new_second = sine * first + cosine * second
                states[layer, odd, half, pl.ds(at + FRONT, STEP), :] = new_first
                states[layer, 1 - odd, half, pl.ds(at + FRONT, STEP), :] = new_second
            return carry

        lax.fori_loop(0, pairs // STEP, block, 0)


def band(states, adjoints, offsets, weights, start, pairs):
    where = []
    for parity in range(2):
        for k in range(BANDS):
            for sign in (1, -1):
                row = parity + sign * offsets[k]
                side = lax.bitwise_and(row, 1)
                where.append((side, lax.shift_right_arithmetic(row, 1) - 1 + side + FRONT + start))

    def block(i, carry):
        at = pl.multiple_of(i * STEP, STEP)
        for parity in range(2):
            for half in range(2):
                total = jnp.zeros((STEP, 128), jnp.float32)
                for k in range(BANDS):
                    side, shift = where[(parity * BANDS + k) * 2]
                    upper = states[LAYERS - 1, side, half, pl.ds(at + shift, STEP), :]
                    side, shift = where[(parity * BANDS + k) * 2 + 1]
                    lower = states[LAYERS - 1, side, half, pl.ds(at + shift, STEP), :]
                    total = total + weights[k] * (upper + lower)
                adjoints[LAYERS - 1, parity, half, pl.ds(at + FRONT, STEP), :] = total
        return carry

    lax.fori_loop(0, pairs // STEP, block, 0)


def backward(states, adjoints, products, cos_sin, table, shift, lead, start, pairs):
    for layer in reversed(range(LAYERS)):
        odd = layer % 2

        def block(i, carry, layer=layer, odd=odd):
            at = pl.multiple_of(i * STEP, STEP)
            angle_at = at + (start + shift) + lead if odd else at + (start + shift)
            cosine = cos_sin[table, layer, pl.ds(angle_at, STEP), :]
            sine = cos_sin[table, LAYERS + layer, pl.ds(angle_at, STEP), :]
            product = None
            for half in range(2):
                if odd:
                    first = adjoints[layer, 1, half, pl.ds(at + FRONT, STEP), :]
                    second = adjoints[layer, 0, half, pl.ds(at + FRONT + 1, STEP), :]
                else:
                    first = adjoints[layer, 0, half, pl.ds(at + FRONT - 1, STEP), :]
                    second = adjoints[layer, 1, half, pl.ds(at + FRONT, STEP), :]
                state_first = states[layer, odd, half, pl.ds(at + start + FRONT, STEP), :]
                state_second = states[layer, 1 - odd, half, pl.ds(at + start + FRONT, STEP), :]
                part = second * state_first - first * state_second
                product = part if product is None else product + part
                if layer:
                    adjoints[layer - 1, odd, half, pl.ds(at + FRONT, STEP), :] = cosine * first + sine * second
                    adjoints[layer - 1, 1 - odd, half, pl.ds(at + FRONT, STEP), :] = cosine * second - sine * first
            products[layer, pl.ds(at + GFRONT, STEP), :] = product
            return carry

        lax.fori_loop(0, pairs // STEP, block, 0)


def summed(products, lead, at):
    rows = []
    for layer in range(LAYERS):
        block = products[layer, pl.ds(at + GFRONT - lead if layer % 2 else at + GFRONT, 128), :]
        rows.append(jnp.sum(jnp.transpose(block), axis=0, keepdims=True))
    return jnp.concatenate(rows, 0)


def inner_kernel(pairing, offsets, weights, slab, angles, evolved, gradient, raw, states, adjoints, products, cos_sin, out, sems):
    loads = []
    for half in range(2):
        loads.append(pltpu.make_async_copy(slab.at[:, pl.ds(128 * half, 128)], raw.at[half, pl.ds(0, ROWS), :], sems.at[half]))
        loads[-1].start()
    lead = pairing[0]
    turn_table(cos_sin, 0, lambda tile: angles[:, 128 * tile : 128 * (tile + 1)], 8)
    for load in loads:
        load.wait()
    forward(raw, states, cos_sin, 0, 0, lead, INNER)

    def weave(i, carry):
        at = pl.multiple_of(i * STEP, STEP)
        for half in range(2):
            out[half, pl.ds(2 * at + lead + FRONT, STEP, stride=2), :] = states[3, 0, half, pl.ds(at + FRONT - 1, STEP), :]
            out[half, pl.ds(2 * at + lead + FRONT + 1, STEP, stride=2), :] = states[3, 1, half, pl.ds(at + FRONT, STEP), :]
        return carry

    lax.fori_loop(0, INNER // STEP, weave, 0)
    stores = []
    for half in range(2):
        stores.append(
            pltpu.make_async_copy(out.at[half, pl.ds(FRONT, ROWS), :], evolved.at[:, pl.ds(128 * half, 128)], sems.at[2 + half])
        )
        stores[-1].start()
    band(states, adjoints, offsets, weights, 256, 512)
    backward(states, adjoints, products, cos_sin, 0, 0, lead, 256, 512)
    for tile in range(4):
        gradient[:, 128 * tile : 128 * (tile + 1)] = summed(products, lead, 128 * tile)
    for store in stores:
        store.wait()


def edge_kernel(
    pairing, offsets, weights, slab, angles, before, after, before_angles, after_angles, inner, evolved_in,
    evolved, gradient, raw, states, adjoints, products, cos_sin, out, sems,
):
    loads = []
    for side in range(2):
        for half in range(2):
            lanes = pl.ds(128 * half, 128)
            if side == 0:
                pieces = [(before, 0, 8, HALO), (slab, 0, 8 + HALO, 2 * EDGE - HALO - 8)]
            else:
                own = 2 * EDGE - HALO - 8
                pieces = [(slab, ROWS - own, 0, own), (after, 0, own, HALO)]
            for source, source_at, at, rows in pieces:
                load = pltpu.make_async_copy(
                    source.at[pl.ds(source_at, rows), lanes],
                    raw.at[side, half, pl.ds(at, rows), :],
                    sems.at[len(loads)],
                )
                load.start()
                loads.append(load)
    lead = pairing[0]

    def left_angles(tile):
        if tile < 3:
            t = tile + 1
            return before_angles[4 * (t // 2) : 4 * (t // 2) + 4, 128 * (t % 2) : 128 * (t % 2) + 128]
        return angles[:, 128 * (tile - 3) : 128 * (tile - 2)]

    def right_angles(tile):
        if tile < 5:
            return angles[:, 128 * (tile + 3) : 128 * (tile + 4)]
        t = tile - 5
        return after_angles[4 * (t // 2) : 4 * (t // 2) + 4, 128 * (t % 2) : 128 * (t % 2) + 128]

    turn_table(cos_sin, 0, left_angles, 8)
    turn_table(cos_sin, 1, right_angles, 8)
    for load in loads:
        load.wait()
    stores = []
    for side in range(2):
        shift = (120, 104)[side]
        forward(raw.at[side], states, cos_sin, side, shift, lead, EDGE)
        at = (256, 528)[side]
        for half in range(2):
            out[side, half, pl.ds(lead, 16, stride=2), :] = states[3, 0, half, pl.ds(at + FRONT - 1, 16), :]
            out[side, half, pl.ds(lead + 1, 16, stride=2), :] = states[3, 1, half, pl.ds(at + FRONT, 16), :]
            store = pltpu.make_async_copy(
                out.at[side, half, pl.ds((16, 8)[side], 8), :],
                evolved.at[pl.ds((0, ROWS - 8)[side], 8), pl.ds(128 * half, 128)],
                sems.at[8 + 2 * side + half],
            )
            store.start()
            stores.append(store)
        band(states, adjoints, offsets, weights, 256, 288)
        backward(states, adjoints, products, cos_sin, side, shift, lead, 256, 288)
        lane = lax.broadcasted_iota(jnp.int32, (LAYERS, 128), 1)
        if side == 0:
            gradient[:, 0:128] = summed(products, lead, 8)
            gradient[:, 128:256] = summed(products, lead, 136)
            gradient[:, 256:384] = jnp.where(lane < 16, summed(products, lead, 264), inner[:, 0:128])
            gradient[:, 384:640] = inner[:, 128:384]
        else:
            gradient[:, 640:768] = jnp.where(lane < 112, inner[:, 384:512], summed(products, lead, -104))
            gradient[:, 768:896] = summed(products, lead, 24)
            gradient[:, 896:1024] = summed(products, lead, 152)
    for store in stores:
        store.wait()


SMALL = pl.BlockSpec(memory_space=pltpu.SMEM)
WHOLE = pl.BlockSpec(memory_space=pltpu.VMEM)
FAR = pl.BlockSpec(memory_space=pl.ANY)


def scratch(sides, rows, pairs, range_pairs, tables, out_shape, sems):
    raw = (2, rows, 128) if sides == 1 else (sides, 2, rows, 128)
    return [
        pltpu.VMEM(raw, jnp.float32),
        pltpu.VMEM((LAYERS, 2, 2, pairs + 2 * FRONT, 128), jnp.float32),
        pltpu.VMEM((LAYERS, 2, 2, range_pairs + 2 * FRONT, 128), jnp.float32),
        pltpu.VMEM((LAYERS, GFRONT + max(range_pairs, 392) + 8, 128), jnp.float32),
        pltpu.VMEM((tables, 2 * LAYERS, 1024 + 8, 128), jnp.float32),
        pltpu.VMEM(out_shape, jnp.float32),
        pltpu.SemaphoreType.DMA((sems,)),
    ]


def inner_call(pairing, offsets, weights, slab, angles):
    return pl.pallas_call(
        inner_kernel,
        out_shape=(jax.ShapeDtypeStruct((ROWS, 256), jnp.float32), jax.ShapeDtypeStruct((LAYERS, 512), jnp.float32)),
        in_specs=[SMALL, SMALL, SMALL, FAR, WHOLE],
        out_specs=(FAR, WHOLE),
        scratch_shapes=scratch(1, ROWS + 8, INNER, 512, 1, (2, ROWS + 2 * FRONT, 128), 4),
        compiler_params=pltpu.CompilerParams(vmem_limit_bytes=40 * 2**20),
        cost_estimate=pl.CostEstimate(flops=40_000_000, bytes_accessed=16 * 2**20, transcendentals=8192),
        name="inner",
    )(pairing, offsets, weights, slab, angles)


def edge_call(pairing, offsets, weights, slab, angles, before, after, before_angles, after_angles, inner, evolved):
    return pl.pallas_call(
        edge_kernel,
        out_shape=(jax.ShapeDtypeStruct((ROWS, 256), jnp.float32), jax.ShapeDtypeStruct((LAYERS, PAIRS), jnp.float32)),
        in_specs=[SMALL, SMALL, SMALL, FAR, WHOLE, FAR, FAR, WHOLE, WHOLE, WHOLE, FAR],
        out_specs=(FAR, WHOLE),
        scratch_shapes=scratch(2, 2 * EDGE + 8, EDGE, 288, 2, (2, 2, 40, 128), 12),
        input_output_aliases={10: 0},
        compiler_params=pltpu.CompilerParams(vmem_limit_bytes=40 * 2**20),
        cost_estimate=pl.CostEstimate(flops=40_000_000, bytes_accessed=16 * 2**20, transcendentals=8192),
        name="edges",
    )(pairing, offsets, weights, slab, angles, before, after, before_angles, after_angles, inner, evolved)


def on_device(slab, angles, pairing, band_offsets, band_weights):
    count = lax.axis_size("blk")
    tail = jnp.concatenate([slab[ROWS - HALO :], angles[:, 512:768], angles[:, 768:]], 0)
    before = lax.ppermute(tail, "blk", [(i, (i + 1) % count) for i in range(count)])
    head = jnp.concatenate([slab[:HALO], angles[:, :256], angles[:, 256:512]], 0)
    after = lax.ppermute(head, "blk", [((i + 1) % count, i) for i in range(count)])
    evolved, inner = inner_call(pairing, band_offsets, band_weights, slab, angles)
    evolved, gradient = edge_call(
        pairing, band_offsets, band_weights, slab, angles, before, after, before[HALO:], after[HALO:], inner, evolved
    )
    columns = lax.axis_size("col")
    step = 1
    while step < columns:
        gradient = gradient + lax.ppermute(gradient, "col", [(i, i ^ step) for i in range(columns)])
        step *= 2
    return (evolved, gradient)


def solution(mesh):
    in_specs = (P("blk", "col"), P(None, "blk"), P(), P(), P())
    out_specs = (P("blk", "col"), P(None, "blk"))
    return jax.shard_map(
        on_device, mesh=mesh, in_specs=in_specs, out_specs=out_specs, check_vma=False
    )
```

```python
import jax
import jax.numpy as jnp
from jax import lax
from jax.experimental import pallas as pl
from jax.experimental.pallas import tpu as pltpu
from jax.sharding import PartitionSpec as P

LAYERS = 4
REACH = 512
BANDS = 8
ROWS = 2048
PAIRS = 1024
NEAR = 280
FAR_ROWS = 240
THIRD = 176
PAD = 272
LENGTH = PAD + PAIRS + PAD
WINDOW = 160
FAR_WINDOW = 136
FRONT = 8
GFRONT = 8
RANGE = 304


def fill_table(table, at, angle, low=0, high=128):
    both = jnp.concatenate([jnp.cos(angle), jnp.sin(angle)], 0)
    tall = jnp.transpose(both)
    for lane in range(2 * LAYERS):
        table[lane, pl.ds(at, high - low), :] = jnp.broadcast_to(tall[low:high, lane : lane + 1], (high - low, 128))


def forward(raw, states, start, table, table_start, lead, pairs, step):
    for layer in range(LAYERS):
        odd = layer % 2

        def block(i, carry, layer=layer, odd=odd):
            at = pl.multiple_of(i * step, 8)
            angle_at = at + table_start + lead if odd else at + table_start
            cosine = table[layer, pl.ds(angle_at, step), :]
            sine = table[LAYERS + layer, pl.ds(angle_at, step), :]
            for half in range(2):
                if layer == 0:
                    first = raw[half, pl.ds(2 * at + lead, step, stride=2), :]
                    second = raw[half, pl.ds(2 * at + lead + 1, step, stride=2), :]
                elif odd:
                    first = states[layer - 1, 1, half, pl.ds(at + start, step), :]
                    second = states[layer - 1, 0, half, pl.ds(at + start + 1, step), :]
                else:
                    first = states[layer - 1, 0, half, pl.ds(at + start - 1, step), :]
                    second = states[layer - 1, 1, half, pl.ds(at + start, step), :]
                states[layer, odd, half, pl.ds(at + start, step), :] = cosine * first - sine * second
                states[layer, 1 - odd, half, pl.ds(at + start, step), :] = sine * first + cosine * second
            return carry

        lax.fori_loop(0, pairs // step, block, 0)


def band(source, source_start, total, total_start, offsets, weights, pairs, step, signs, add):
    where = []
    for parity in range(2):
        for k in range(BANDS):
            for sign in signs:
                row = parity + sign * offsets[k]
                side = lax.bitwise_and(row, 1)
                where.append((side, lax.shift_right_arithmetic(row, 1) - 1 + side + source_start))

    def block(i, carry):
        at = pl.multiple_of(i * step, 8)
        for parity in range(2):
            for half in range(2):
                place = (parity, half, pl.ds(at + total_start, step), slice(None))
                value = total[place] if add else None
                for k in range(BANDS):
                    term = None
                    for n in range(len(signs)):
                        side, shift = where[(parity * BANDS + k) * len(signs) + n]
                        row = source[side, half, pl.ds(at + shift, step), :]
                        term = row if term is None else term + row
                    term = weights[k] * term
                    value = term if value is None else value + term
                total[place] = value
        return carry

    lax.fori_loop(0, pairs // step, block, 0)


def backward(states, start, adjoint, adjoint_start, turned, products, table, table_start, lead, pairs, step):
    for layer in reversed(range(LAYERS)):
        odd = layer % 2

        def block(i, carry, layer=layer, odd=odd):
            at = pl.multiple_of(i * step, 8)
            angle_at = at + table_start + lead if odd else at + table_start
            cosine = table[layer, pl.ds(angle_at, step), :]
            sine = table[LAYERS + layer, pl.ds(angle_at, step), :]
            product = None
            for half in range(2):
                source = adjoint if layer == LAYERS - 1 else turned.at[layer]
                begin = adjoint_start if layer == LAYERS - 1 else FRONT
                if odd:
                    first = source[1, half, pl.ds(at + begin, step), :]
                    second = source[0, half, pl.ds(at + begin + 1, step), :]
                else:
                    first = source[0, half, pl.ds(at + begin - 1, step), :]
                    second = source[1, half, pl.ds(at + begin, step), :]
                state_first = states[layer, odd, half, pl.ds(at + start, step), :]
                state_second = states[layer, 1 - odd, half, pl.ds(at + start, step), :]
                part = second * state_first - first * state_second
                product = part if product is None else product + part
                if layer:
                    turned[layer - 1, odd, half, pl.ds(at + FRONT, step), :] = cosine * first + sine * second
                    turned[layer - 1, 1 - odd, half, pl.ds(at + FRONT, step), :] = cosine * second - sine * first
            products[layer, pl.ds(at + GFRONT, step), :] = product
            return carry

        lax.fori_loop(0, pairs // step, block, 0)


def summed(products, lead, at):
    rows = []
    for layer in range(LAYERS):
        block = products[layer, pl.ds(at + GFRONT - lead if layer % 2 else at + GFRONT, 128), :]
        rows.append(jnp.sum(jnp.transpose(block), axis=0, keepdims=True))
    return jnp.concatenate(rows, 0)


def inner_kernel(
    pairing, offsets, weights, slab, angles,
    evolved, states, adjoint, table, gradient, raw, turned, products, out, sems,
):
    loads = []
    for half in range(2):
        loads.append(pltpu.make_async_copy(slab.at[:, pl.ds(128 * half, 128)], raw.at[half, pl.ds(0, ROWS), :], sems.at[half]))
        loads[-1].start()
    lead = pairing[0]
    for tile in range(8):
        fill_table(table, FRONT + 128 * tile, angles[:, 128 * tile : 128 * (tile + 1)])
    for load in loads:
        load.wait()
    forward(raw, states, PAD, table, FRONT, lead, PAIRS, 128)

    def weave(i, carry):
        at = pl.multiple_of(i * 128, 128)
        for half in range(2):
            out[half, pl.ds(2 * at + lead + FRONT, 128, stride=2), :] = states[3, 0, half, pl.ds(at + PAD - 1, 128), :]
            out[half, pl.ds(2 * at + lead + FRONT + 1, 128, stride=2), :] = states[3, 1, half, pl.ds(at + PAD, 128), :]
        return carry

    lax.fori_loop(0, PAIRS // 128, weave, 0)
    stores = []
    for half in range(2):
        stores.append(
            pltpu.make_async_copy(out.at[half, pl.ds(FRONT, ROWS), :], evolved.at[:, pl.ds(128 * half, 128)], sems.at[2 + half])
        )
        stores[-1].start()
    blank = jnp.zeros((PAD + 8, 128), jnp.float32)
    last = states.at[LAYERS - 1]
    for parity in range(2):
        for half in range(2):
            last[parity, half, pl.ds(0, PAD + 8), :] = blank
            last[parity, half, pl.ds(PAD + PAIRS - 8, PAD + 8), :] = blank
    band(last, PAD - 8, adjoint, FRONT, offsets, weights, PAIRS + 16, 104, (1, -1), False)
    backward(states, PAD + 256, adjoint, FRONT + 8 + 256, turned, products, table, FRONT + 256, lead, 512, 128)
    for tile in range(4):
        gradient[:, 128 * tile : 128 * (tile + 1)] = summed(products, lead, 128 * tile)
    for store in stores:
        store.wait()


def halo_angles(halo, at, tile):
    return halo[at + 4 * (tile // 2) : at + 4 * (tile // 2) + 4, 128 * (tile % 2) : 128 * (tile % 2) + 128]


def started(pieces, raw, sems):
    loads = []
    for half in range(2):
        for piece, piece_at, at, rows in pieces:
            load = pltpu.make_async_copy(
                piece.at[pl.ds(piece_at, rows), pl.ds(128 * half, 128)], raw.at[half, pl.ds(at, rows), :], sems.at[len(loads)]
            )
            load.start()
            loads.append(load)
    return loads


def near_tables(side, halo, at, table, halo_table):
    if side == 0:
        fill_table(halo_table, 0, halo_angles(halo, at, 1), 120, 128)
        fill_table(halo_table, 8, halo_angles(halo, at, 2))
        fill_table(halo_table, 136, halo_angles(halo, at, 3))
    else:
        fill_table(halo_table, 16, halo_angles(halo, at, 0))
        fill_table(halo_table, 144, halo_angles(halo, at, 1))
        fill_table(halo_table, 272, halo_angles(halo, at, 2), 0, 16)
    for lane in range(2 * LAYERS):
        if side == 0:
            halo_table[lane, pl.ds(264, 24), :] = table[lane, pl.ds(FRONT, 24), :]
            table[lane, pl.ds(0, FRONT), :] = halo_table[lane, pl.ds(256, 8), :]
        else:
            halo_table[lane, pl.ds(0, 16), :] = table[lane, pl.ds(FRONT + PAIRS - 16, 16), :]
            table[lane, pl.ds(FRONT + PAIRS, 16), :] = halo_table[lane, pl.ds(16, 16), :]


def near_side(
    side, lead, offsets, weights, raw, window, source, states, adjoint, table, halo_table, turned, products, out, evolved, sems
):
    forward(raw, window, FRONT, halo_table, (120, 0)[side], lead, WINDOW, 80)
    stores = []
    blank = jnp.zeros((272, 128), jnp.float32)
    at = FRONT + (144, 8)[side]
    for half in range(2):
        out[half, pl.ds(lead, 16, stride=2), :] = window[3, 0, half, pl.ds(at - 9, 16), :]
        out[half, pl.ds(lead + 1, 16, stride=2), :] = window[3, 1, half, pl.ds(at - 8, 16), :]
        store = pltpu.make_async_copy(
            out.at[half, pl.ds(16, 16), :],
            evolved.at[pl.ds((0, ROWS - 16)[side], 16), pl.ds(128 * half, 128)],
            sems.at[half],
        )
        store.start()
        stores.append(store)
        for parity in range(2):
            for layer in range(LAYERS):
                states[layer, parity, half, pl.ds(PAD + (-8, PAIRS - 8)[side], 16), :] = window[
                    layer, parity, half, pl.ds(at + (-8, 0)[side], 16), :
                ]
            if side == 0:
                source[parity, half, pl.ds(0, 136), :] = blank[:136]
                source[parity, half, pl.ds(136, 144), :] = window[3, parity, half, pl.ds(FRONT + 8, 144), :]
                source[parity, half, pl.ds(280, 272), :] = blank
            else:
                source[parity, half, pl.ds(0, 272), :] = blank
                source[parity, half, pl.ds(272, 144), :] = window[3, parity, half, pl.ds(FRONT + 8, 144), :]
                source[parity, half, pl.ds(416, 128), :] = blank[:128]
    band(source, (264, 0)[side], adjoint, FRONT + (0, 752)[side], offsets, weights, 288, 96, ((-1,), (1,))[side], True)
    band(source, (264, 272)[side], adjoint, FRONT + (0, PAIRS)[side], offsets, weights, 16, 16, ((1,), (-1,))[side], True)
    begin = (120, 744)[side]
    backward(states, PAD + begin, adjoint, FRONT + 8 + begin, turned, products, table, FRONT + begin, lead, 160, 80)
    return stores


def far_side(side, lead, offsets, weights, raw, window, source, states, adjoint, table, halo_table, turned, products):
    forward(raw, window, FRONT, halo_table, (0, 144)[side], lead, FAR_WINDOW, 136)
    blank = jnp.zeros((272, 128), jnp.float32)
    for parity in range(2):
        for half in range(2):
            value = window[3, parity, half, pl.ds(FRONT + (0, 8)[side], 128), :]
            if side == 0:
                source[parity, half, pl.ds(8, 128), :] = value
                source[parity, half, pl.ds(136, 272), :] = blank
            else:
                source[parity, half, pl.ds(0, 272), :] = blank
                source[parity, half, pl.ds(272, 128), :] = value
    band(source, (264, 0)[side], adjoint, FRONT + (0, 896)[side], offsets, weights, 144, 144, ((-1,), (1,))[side], True)
    begin = (-8, 888)[side]
    backward(states, PAD + begin, adjoint, FRONT + 8 + begin, turned, products, table, FRONT + begin, lead, 144, 144)


def left_kernel(
    pairing, offsets, weights, slab, before, evolved_in, states_in, adjoint_in, table_in, inner,
    evolved, states, adjoint, table, halo_table, gradient, raw, window, source, turned, products, out, sems,
):
    loads = started(((before, 0, 8, NEAR), (slab, 0, 8 + NEAR, 40)), raw, sems)
    lead = pairing[0]
    near_tables(0, before, NEAR, table, halo_table)
    for load in loads:
        load.wait()
    stores = near_side(
        0, lead, offsets, weights, raw, window, source, states, adjoint, table, halo_table, turned, products, out, evolved,
        sems.at[pl.ds(4, 2)],
    )
    lane = lax.broadcasted_iota(jnp.int32, (LAYERS, 128), 1)
    gradient[:, 0:128] = summed(products, lead, 8)
    gradient[:, 128:256] = jnp.where(lane < 16, summed(products, lead, 136), inner[:, 0:128])
    gradient[:, 256:512] = inner[:, 128:384]
    for store in stores:
        store.wait()


def rest_kernel(
    pairing, offsets, weights, slab, before, before_far, after, after_next, after_last, left_table, inner, left,
    evolved_in, states_in, adjoint_in, table_in,
    evolved, states, adjoint, table, gradient, raw, raw_left, raw_right, window, source, turned, products, right_table, out, sems,
):
    loads = started(
        ((slab, ROWS - 32, 0, 32), (after, 0, 32, THIRD), (after_next, 0, 32 + THIRD, NEAR - THIRD)), raw, sems
    )
    loads_left = started(((before_far, 0, 8, FAR_ROWS), (before, 0, 8 + FAR_ROWS, 32)), raw_left, sems.at[pl.ds(6, 4)])
    loads_right = started(
        ((after_next, NEAR - 24 - THIRD, 0, 2 * THIRD + 24 - NEAR), (after_last, 0, 2 * THIRD + 24 - NEAR, THIRD - 8)),
        raw_right,
        sems.at[pl.ds(10, 4)],
    )
    lead = pairing[0]
    near_tables(1, after_last, THIRD - 8, table, right_table)
    for load in loads:
        load.wait()
    common = (window, source, states, adjoint, table)
    stores = near_side(
        1, lead, offsets, weights, raw, *common, right_table, turned, products, out, evolved, sems.at[pl.ds(14, 2)]
    )
    lane = lax.broadcasted_iota(jnp.int32, (LAYERS, 128), 1)
    gradient[:, 128:640] = left[...]
    gradient[:, 640:768] = jnp.where(lane < 112, inner[:, 384:512], pltpu.roll(summed(products, lead, 8), 112, 1))
    gradient[:, 768:896] = summed(products, lead, 24)
    for load in loads_left:
        load.wait()
    far_side(0, lead, offsets, weights, raw_left, *common, left_table, turned, products)
    gradient[:, 0:128] = summed(products, lead, 8)
    for load in loads_right:
        load.wait()
    far_side(1, lead, offsets, weights, raw_right, *common, right_table, turned, products)
    gradient[:, 896:1024] = summed(products, lead, 8)
    for store in stores:
        store.wait()


SMALL = pl.BlockSpec(memory_space=pltpu.SMEM)
WHOLE = pl.BlockSpec(memory_space=pltpu.VMEM)
FAR = pl.BlockSpec(memory_space=pl.ANY)

EVOLVED = jax.ShapeDtypeStruct((ROWS, 256), jnp.float32)
STATES = jax.ShapeDtypeStruct((LAYERS, 2, 2, LENGTH, 128), jnp.float32)
ADJOINT = jax.ShapeDtypeStruct((2, 2, PAIRS + 32, 128), jnp.float32)
TABLE = jax.ShapeDtypeStruct((2 * LAYERS, PAIRS + 32, 128), jnp.float32)
HALO_TABLE = jax.ShapeDtypeStruct((2 * LAYERS, 296, 128), jnp.float32)


def limits(flops, traffic, grant=16):
    return dict(
        compiler_params=pltpu.CompilerParams(vmem_limit_bytes=grant * 2**20),
        cost_estimate=pl.CostEstimate(flops=flops, bytes_accessed=traffic, transcendentals=8192),
    )


def room(*shape):
    return pltpu.VMEM(shape, jnp.float32)


def pack_call(slab, angles, pieces, angle_at, *earlier):
    def kernel(slab, angles, *refs):
        packed, tiles, sems = refs[len(earlier) : len(earlier) + len(pieces)], refs[-2], refs[-1]
        copies = [pltpu.make_async_copy(angles, tiles, sems.at[len(pieces)])]
        for n, (first, rows, _) in enumerate(pieces):
            copies.append(
                pltpu.make_async_copy(slab.at[pl.ds(first, rows), :], packed[n].at[pl.ds(0, rows), :], sems.at[n])
            )
        for copy in copies:
            copy.start()
        copies[0].wait()
        for n, (_, rows, follow) in enumerate(pieces):
            for row in range(2 * follow):
                lanes = slice(angle_at + 256 * row, angle_at + 256 * (row + 1))
                packed[n][rows + 4 * row : rows + 4 * (row + 1), :] = tiles[:, lanes]
        for copy in copies[1:]:
            copy.wait()

    slab = pltpu.with_memory_space_constraint(slab, pltpu.HBM)
    angles = pltpu.with_memory_space_constraint(angles, pltpu.HBM)
    return pl.pallas_call(
        kernel,
        out_shape=[jax.ShapeDtypeStruct((rows + 8 * follow, 256), jnp.float32) for _, rows, follow in pieces],
        in_specs=[pl.BlockSpec(memory_space=pltpu.HBM)] * 2 + [FAR] * len(earlier),
        out_specs=[WHOLE] * len(pieces),
        scratch_shapes=[room(LAYERS, PAIRS), pltpu.SemaphoreType.DMA((len(pieces) + 1,))],
        name="pack",
        **limits(1000, 2**20),
    )(slab, angles, *earlier)


def inner_call(pairing, offsets, weights, slab, angles):
    return pl.pallas_call(
        inner_kernel,
        out_shape=(EVOLVED, STATES, ADJOINT, TABLE, jax.ShapeDtypeStruct((LAYERS, 512), jnp.float32)),
        in_specs=[SMALL, SMALL, SMALL, FAR, WHOLE],
        out_specs=(FAR, WHOLE, WHOLE, WHOLE, WHOLE),
        scratch_shapes=[
            room(2, ROWS + 8, 128),
            room(LAYERS - 1, 2, 2, 512 + 16, 128),
            room(LAYERS, 512 + 16, 128),
            room(2, ROWS + 16, 128),
            pltpu.SemaphoreType.DMA((4,)),
        ],
        name="inner",
        **limits(60_000_000, 24 * 2**20),
    )(pairing, offsets, weights, slab, angles)


def left_call(pairing, offsets, weights, slab, before, evolved, states, adjoint, table, inner):
    return pl.pallas_call(
        left_kernel,
        out_shape=(EVOLVED, STATES, ADJOINT, TABLE, HALO_TABLE, jax.ShapeDtypeStruct((LAYERS, 512), jnp.float32)),
        in_specs=[SMALL, SMALL, SMALL, FAR, WHOLE, FAR, WHOLE, WHOLE, WHOLE, WHOLE],
        out_specs=(FAR, WHOLE, WHOLE, WHOLE, WHOLE, WHOLE),
        scratch_shapes=[
            room(2, 328, 128),
            room(LAYERS, 2, 2, WINDOW + 16, 128),
            room(2, 2, 552, 128),
            room(LAYERS - 1, 2, 2, 160 + 16, 128),
            room(LAYERS, 280, 128),
            room(2, 40, 128),
            pltpu.SemaphoreType.DMA((6,)),
        ],
        input_output_aliases={5: 0, 6: 1, 7: 2, 8: 3},
        name="left",
        **limits(15_000_000, 8 * 2**20),
    )(pairing, offsets, weights, slab, before, evolved, states, adjoint, table, inner)


def rest_call(*operands):
    return pl.pallas_call(
        rest_kernel,
        out_shape=(EVOLVED, STATES, ADJOINT, TABLE, jax.ShapeDtypeStruct((LAYERS, PAIRS), jnp.float32)),
        in_specs=[SMALL, SMALL, SMALL, FAR] + [WHOLE] * 8 + [FAR, WHOLE, WHOLE, WHOLE],
        out_specs=(FAR, WHOLE, WHOLE, WHOLE, WHOLE),
        scratch_shapes=[
            room(2, 328, 128),
            room(2, 280, 128),
            room(2, 280, 128),
            room(LAYERS, 2, 2, WINDOW + 16, 128),
            room(2, 2, 552, 128),
            room(LAYERS - 1, 2, 2, 160 + 16, 128),
            room(LAYERS, 280, 128),
            room(2 * LAYERS, 296, 128),
            room(2, 40, 128),
            pltpu.SemaphoreType.DMA((16,)),
        ],
        input_output_aliases={12: 0, 13: 1, 14: 2, 15: 3},
        name="rest",
        **limits(30_000_000, 8 * 2**20),
    )(*operands)


def on_device(slab, angles, pairing, band_offsets, band_weights):
    count = lax.axis_size("blk")
    onward = [(i, (i + 1) % count) for i in range(count)]
    back = [((i + 1) % count, i) for i in range(count)]
    tail, far_tail = pack_call(
        slab, angles, ((ROWS - NEAR, NEAR, 1), (ROWS - NEAR - FAR_ROWS, FAR_ROWS, 0)), 512
    )
    before = lax.ppermute(tail, "blk", onward)
    before_far = lax.ppermute(far_tail, "blk", onward)
    heads = pack_call(slab, angles, ((0, THIRD, 0), (THIRD, THIRD, 0), (2 * THIRD, THIRD - 8, 1)), 0, far_tail)
    after = [lax.ppermute(head, "blk", back) for head in heads]
    scalars = (pairing, band_offsets, band_weights)
    evolved, states, adjoint, table, gradient = inner_call(*scalars, slab, angles)
    evolved, states, adjoint, table, left_table, left = left_call(
        *scalars, slab, before, evolved, states, adjoint, table, gradient
    )
    evolved, _, _, _, gradient = rest_call(
        *scalars, slab, before, before_far, *after, left_table, gradient, left, evolved, states, adjoint, table
    )
    columns = lax.axis_size("col")
    step = 1
    while step < columns:
        gradient = gradient + lax.ppermute(gradient, "col", [(i, i ^ step) for i in range(columns)])
        step *= 2
    return (evolved, gradient)


def solution(mesh):
    in_specs = (P("blk", "col"), P(None, "blk"), P(), P(), P())
    out_specs = (P("blk", "col"), P(None, "blk"))
    return jax.shard_map(
        on_device, mesh=mesh, in_specs=in_specs, out_specs=out_specs, check_vma=False
    )
```

```python
import jax
import jax.numpy as jnp
from jax import lax
from jax.experimental import pallas as pl
from jax.experimental.pallas import tpu as pltpu
from jax.sharding import PartitionSpec as P

LAYERS = 4
REACH = 512
BANDS = 8
ROWS = 2048
PAIRS = 1024
NEAR = 280
FAR_ROWS = 240
HALO = NEAR + FAR_ROWS
SENT = NEAR + 8
PAD = 272
LENGTH = PAD + PAIRS + PAD
WINDOW = 160
FAR_WINDOW = 136
FULL_WINDOW = 288
FRONT = 8
GFRONT = 8


def fill_table(table, at, angle, low=0, high=128):
    both = jnp.concatenate([jnp.cos(angle), jnp.sin(angle)], 0)
    tall = jnp.transpose(both)
    for lane in range(2 * LAYERS):
        table[lane, pl.ds(at, high - low), :] = jnp.broadcast_to(tall[low:high, lane : lane + 1], (high - low, 128))


def forward(raw, states, start, table, table_start, lead, pairs, step):
    for layer in range(LAYERS):
        odd = layer % 2

        def block(i, carry, layer=layer, odd=odd):
            at = pl.multiple_of(i * step, 8)
            angle_at = at + table_start + lead if odd else at + table_start
            cosine = table[layer, pl.ds(angle_at, step), :]
            sine = table[LAYERS + layer, pl.ds(angle_at, step), :]
            for half in range(2):
                if layer == 0:
                    first = raw[half, pl.ds(2 * at + lead, step, stride=2), :]
                    second = raw[half, pl.ds(2 * at + lead + 1, step, stride=2), :]
                elif odd:
                    first = states[layer - 1, 1, half, pl.ds(at + start, step), :]
                    second = states[layer - 1, 0, half, pl.ds(at + start + 1, step), :]
                else:
                    first = states[layer - 1, 0, half, pl.ds(at + start - 1, step), :]
                    second = states[layer - 1, 1, half, pl.ds(at + start, step), :]
                states[layer, odd, half, pl.ds(at + start, step), :] = cosine * first - sine * second
                states[layer, 1 - odd, half, pl.ds(at + start, step), :] = sine * first + cosine * second
            return carry

        lax.fori_loop(0, pairs // step, block, 0)


def band(source, source_start, total, total_start, offsets, weights, pairs, step, signs, add):
    where = []
    for parity in range(2):
        for k in range(BANDS):
            for sign in signs:
                row = parity + sign * offsets[k]
                side = lax.bitwise_and(row, 1)
                where.append((side, lax.shift_right_arithmetic(row, 1) - 1 + side + source_start))

    def block(i, carry):
        at = pl.multiple_of(i * step, 8)
        for parity in range(2):
            for half in range(2):
                place = (parity, half, pl.ds(at + total_start, step), slice(None))
                value = total[place] if add else None
                for k in range(BANDS):
                    term = None
                    for n in range(len(signs)):
                        side, shift = where[(parity * BANDS + k) * len(signs) + n]
                        row = source[side, half, pl.ds(at + shift, step), :]
                        term = row if term is None else term + row
                    term = weights[k] * term
                    value = term if value is None else value + term
                total[place] = value
        return carry

    lax.fori_loop(0, pairs // step, block, 0)


def backward(states, start, adjoint, adjoint_start, turned, products, table, table_start, lead, pairs, step):
    for layer in reversed(range(LAYERS)):
        odd = layer % 2

        def block(i, carry, layer=layer, odd=odd):
            at = pl.multiple_of(i * step, 8)
            angle_at = at + table_start + lead if odd else at + table_start
            cosine = table[layer, pl.ds(angle_at, step), :]
            sine = table[LAYERS + layer, pl.ds(angle_at, step), :]
            product = None
            for half in range(2):
                source = adjoint if layer == LAYERS - 1 else turned.at[layer]
                begin = adjoint_start if layer == LAYERS - 1 else FRONT
                if odd:
                    first = source[1, half, pl.ds(at + begin, step), :]
                    second = source[0, half, pl.ds(at + begin + 1, step), :]
                else:
                    first = source[0, half, pl.ds(at + begin - 1, step), :]
                    second = source[1, half, pl.ds(at + begin, step), :]
                state_first = states[layer, odd, half, pl.ds(at + start, step), :]
                state_second = states[layer, 1 - odd, half, pl.ds(at + start, step), :]
                part = second * state_first - first * state_second
                product = part if product is None else product + part
                if layer:
                    turned[layer - 1, odd, half, pl.ds(at + FRONT, step), :] = cosine * first + sine * second
                    turned[layer - 1, 1 - odd, half, pl.ds(at + FRONT, step), :] = cosine * second - sine * first
            products[layer, pl.ds(at + GFRONT, step), :] = product
            return carry

        lax.fori_loop(0, pairs // step, block, 0)


def summed(products, lead, at):
    rows = []
    for layer in range(LAYERS):
        block = products[layer, pl.ds(at + GFRONT - lead if layer % 2 else at + GFRONT, 128), :]
        rows.append(jnp.sum(jnp.transpose(block), axis=0, keepdims=True))
    return jnp.concatenate(rows, 0)


def inner_kernel(
    pairing, offsets, weights, slab, angles,
    evolved, states, adjoint, table, gradient, raw, turned, products, out, sems,
):
    loads = []
    for half in range(2):
        loads.append(pltpu.make_async_copy(slab.at[:, pl.ds(128 * half, 128)], raw.at[half, pl.ds(0, ROWS), :], sems.at[half]))
        loads[-1].start()
    lead = pairing[0]
    for tile in range(8):
        fill_table(table, FRONT + 128 * tile, angles[:, 128 * tile : 128 * (tile + 1)])
    for load in loads:
        load.wait()
    forward(raw, states, PAD, table, FRONT, lead, PAIRS, 128)

    def weave(i, carry):
        at = pl.multiple_of(i * 128, 128)
        for half in range(2):
            out[half, pl.ds(2 * at + lead + FRONT, 128, stride=2), :] = states[3, 0, half, pl.ds(at + PAD - 1, 128), :]
            out[half, pl.ds(2 * at + lead + FRONT + 1, 128, stride=2), :] = states[3, 1, half, pl.ds(at + PAD, 128), :]
        return carry

    lax.fori_loop(0, PAIRS // 128, weave, 0)
    stores = []
    for half in range(2):
        stores.append(
            pltpu.make_async_copy(out.at[half, pl.ds(FRONT, ROWS), :], evolved.at[:, pl.ds(128 * half, 128)], sems.at[2 + half])
        )
        stores[-1].start()
    blank = jnp.zeros((PAD + 8, 128), jnp.float32)
    last = states.at[LAYERS - 1]
    for parity in range(2):
        for half in range(2):
            last[parity, half, pl.ds(0, PAD + 8), :] = blank
            last[parity, half, pl.ds(PAD + PAIRS - 8, PAD + 8), :] = blank
    band(last, PAD - 8, adjoint, FRONT, offsets, weights, PAIRS + 16, 104, (1, -1), False)
    backward(states, PAD + 256, adjoint, FRONT + 8 + 256, turned, products, table, FRONT + 256, lead, 512, 128)
    for tile in range(4):
        gradient[:, 128 * tile : 128 * (tile + 1)] = summed(products, lead, 128 * tile)
    for store in stores:
        store.wait()


def halo_angles(halo, at, tile):
    return halo[at + 4 * (tile // 2) : at + 4 * (tile // 2) + 4, 128 * (tile % 2) : 128 * (tile % 2) + 128]


def started(pieces, raw, sems):
    loads = []
    for half in range(2):
        for piece, piece_at, at, rows in pieces:
            load = pltpu.make_async_copy(
                piece.at[pl.ds(piece_at, rows), pl.ds(128 * half, 128)], raw.at[half, pl.ds(at, rows), :], sems.at[len(loads)]
            )
            load.start()
            loads.append(load)
    return loads


def near_tables(side, halo, at, table, halo_table):
    if side == 0:
        fill_table(halo_table, 0, halo_angles(halo, at, 1), 120, 128)
        fill_table(halo_table, 8, halo_angles(halo, at, 2))
        fill_table(halo_table, 136, halo_angles(halo, at, 3))
    else:
        fill_table(halo_table, 16, halo_angles(halo, at, 0))
        fill_table(halo_table, 144, halo_angles(halo, at, 1))
        fill_table(halo_table, 272, halo_angles(halo, at, 2), 0, 16)
    for lane in range(2 * LAYERS):
        if side == 0:
            halo_table[lane, pl.ds(264, 24), :] = table[lane, pl.ds(FRONT, 24), :]
            table[lane, pl.ds(0, FRONT), :] = halo_table[lane, pl.ds(256, 8), :]
        else:
            halo_table[lane, pl.ds(0, 16), :] = table[lane, pl.ds(FRONT + PAIRS - 16, 16), :]
            table[lane, pl.ds(FRONT + PAIRS, 16), :] = halo_table[lane, pl.ds(16, 16), :]


def boundary(side, at, lead, window, states, out, evolved, sems):
    stores = []
    for half in range(2):
        out[half, pl.ds(lead, 16, stride=2), :] = window[3, 0, half, pl.ds(at - 9, 16), :]
        out[half, pl.ds(lead + 1, 16, stride=2), :] = window[3, 1, half, pl.ds(at - 8, 16), :]
        store = pltpu.make_async_copy(
            out.at[half, pl.ds(16, 16), :],
            evolved.at[pl.ds((0, ROWS - 16)[side], 16), pl.ds(128 * half, 128)],
            sems.at[half],
        )
        store.start()
        stores.append(store)
        for parity in range(2):
            for layer in range(LAYERS):
                states[layer, parity, half, pl.ds(PAD + (-8, PAIRS - 8)[side], 16), :] = window[
                    layer, parity, half, pl.ds(at + (-8, 0)[side], 16), :
                ]
    return stores


def left_kernel(
    pairing, offsets, weights, slab, before, evolved_in, states_in, adjoint_in, table_in, inner,
    evolved, states, adjoint, table, halo_table, gradient, raw, window, source, turned, products, out, sems,
):
    loads = started(((before, 0, 8, NEAR), (slab, 0, 8 + NEAR, 40)), raw, sems)
    lead = pairing[0]
    near_tables(0, before, NEAR, table, halo_table)
    for load in loads:
        load.wait()
    forward(raw, window, FRONT, halo_table, 120, lead, WINDOW, 80)
    stores = boundary(0, FRONT + 144, lead, window, states, out, evolved, sems.at[pl.ds(4, 2)])
    blank = jnp.zeros((272, 128), jnp.float32)
    for half in range(2):
        for parity in range(2):
            source[parity, half, pl.ds(0, 136), :] = blank[:136]
            source[parity, half, pl.ds(136, 144), :] = window[3, parity, half, pl.ds(FRONT + 8, 144), :]
            source[parity, half, pl.ds(280, 272), :] = blank
    band(source, 264, adjoint, FRONT, offsets, weights, 288, 96, (-1,), True)
    band(source, 264, adjoint, FRONT, offsets, weights, 16, 16, (1,), True)
    backward(states, PAD + 120, adjoint, FRONT + 8 + 120, turned, products, table, FRONT + 120, lead, 160, 80)
    lane = lax.broadcasted_iota(jnp.int32, (LAYERS, 128), 1)
    gradient[:, 0:128] = summed(products, lead, 8)
    gradient[:, 128:256] = jnp.where(lane < 16, summed(products, lead, 136), inner[:, 0:128])
    gradient[:, 256:512] = inner[:, 128:384]
    for store in stores:
        store.wait()


def left_far_kernel(
    pairing, offsets, weights, before, before_far, states, table, halo_table, rest, adjoint_in,
    adjoint, gradient, raw, window, source, turned, products, sems,
):
    loads = started(((before_far, SENT - FAR_ROWS, 8, FAR_ROWS), (before, 0, 8 + FAR_ROWS, 32)), raw, sems)
    lead = pairing[0]
    blank = jnp.zeros((272, 128), jnp.float32)
    for half in range(2):
        for parity in range(2):
            source[parity, half, pl.ds(136, 272), :] = blank
    gradient[:, 128:1024] = rest[...]
    for load in loads:
        load.wait()
    forward(raw, window, FRONT, halo_table, 0, lead, FAR_WINDOW, 136)
    for half in range(2):
        for parity in range(2):
            source[parity, half, pl.ds(8, 128), :] = window[3, parity, half, pl.ds(FRONT, 128), :]
    band(source, 264, adjoint, FRONT, offsets, weights, 144, 144, (-1,), True)
    backward(states, PAD - 8, adjoint, FRONT, turned, products, table, FRONT - 8, lead, 144, 144)
    gradient[:, 0:128] = summed(products, lead, 8)


def right_kernel(
    pairing, offsets, weights, slab, after, after_far, inner, left, evolved_in, states_in, adjoint_in, table_in,
    evolved, states, adjoint, table, gradient, raw, window, source, turned, products, halo_table, out, sems,
):
    loads = started(
        ((slab, ROWS - 32, 0, 32), (after, 0, 32, NEAR), (after_far, 0, 32 + NEAR, FAR_ROWS)), raw, sems
    )
    lead = pairing[0]
    near_tables(1, after, NEAR, table, halo_table)
    blank = jnp.zeros((272, 128), jnp.float32)
    for half in range(2):
        for parity in range(2):
            source[parity, half, pl.ds(0, 272), :] = blank
    gradient[:, 0:512] = left[...]
    for load in loads:
        load.wait()
    forward(raw, window, FRONT, halo_table, 0, lead, FULL_WINDOW, 144)
    stores = boundary(1, FRONT + 8, lead, window, states, out, evolved, sems.at[pl.ds(6, 2)])
    for half in range(2):
        for parity in range(2):
            source[parity, half, pl.ds(272, 280), :] = window[3, parity, half, pl.ds(FRONT + 8, 280), :]
    band(source, 0, adjoint, FRONT + 752, offsets, weights, 288, 144, (1,), True)
    band(source, 272, adjoint, FRONT + PAIRS, offsets, weights, 16, 16, (-1,), True)
    backward(states, PAD + 744, adjoint, FRONT + 8 + 744, turned, products, table, FRONT + 744, lead, 288, 144)
    lane = lax.broadcasted_iota(jnp.int32, (LAYERS, 128), 1)
    gradient[:, 512:640] = jnp.where(lane < 112, inner[:, 384:512], pltpu.roll(summed(products, lead, 8), 112, 1))
    gradient[:, 640:768] = summed(products, lead, 24)
    gradient[:, 768:896] = summed(products, lead, 152)
    for store in stores:
        store.wait()


SMALL = pl.BlockSpec(memory_space=pltpu.SMEM)
WHOLE = pl.BlockSpec(memory_space=pltpu.VMEM)
FAR = pl.BlockSpec(memory_space=pl.ANY)

EVOLVED = jax.ShapeDtypeStruct((ROWS, 256), jnp.float32)
STATES = jax.ShapeDtypeStruct((LAYERS, 2, 2, LENGTH, 128), jnp.float32)
ADJOINT = jax.ShapeDtypeStruct((2, 2, PAIRS + 32, 128), jnp.float32)
TABLE = jax.ShapeDtypeStruct((2 * LAYERS, PAIRS + 32, 128), jnp.float32)
HALO_TABLE = jax.ShapeDtypeStruct((2 * LAYERS, 304, 128), jnp.float32)


def limits(flops, traffic, grant=16):
    return dict(
        compiler_params=pltpu.CompilerParams(vmem_limit_bytes=grant * 2**20),
        cost_estimate=pl.CostEstimate(flops=flops, bytes_accessed=traffic, transcendentals=8192),
    )


def room(*shape):
    return pltpu.VMEM(shape, jnp.float32)


def pack_call(slab, angles, pieces, *earlier):
    shapes = [(rows + (0 if lane is None else 8), 256) for _, rows, lane in pieces]

    def kernel(slab, angles, *refs):
        packed, tiles, sems = refs[len(earlier) : len(earlier) + len(pieces)], refs[-2], refs[-1]
        copies = [pltpu.make_async_copy(angles, tiles, sems.at[len(pieces)])]
        for n, (first, rows, _) in enumerate(pieces):
            copies.append(
                pltpu.make_async_copy(slab.at[pl.ds(first, rows), :], packed[n].at[pl.ds(0, rows), :], sems.at[n])
            )
        for copy in copies:
            copy.start()
        copies[0].wait()
        for n, (_, rows, lane) in enumerate(pieces):
            if lane is not None:
                for row in range(2):
                    lanes = slice(lane + 256 * row, lane + 256 * (row + 1))
                    packed[n][rows + 4 * row : rows + 4 * (row + 1), :] = tiles[:, lanes]
        for copy in copies[1:]:
            copy.wait()

    slab = pltpu.with_memory_space_constraint(slab, pltpu.HBM)
    angles = pltpu.with_memory_space_constraint(angles, pltpu.HBM)
    return pl.pallas_call(
        kernel,
        out_shape=[jax.ShapeDtypeStruct(shape, jnp.float32) for shape in [*shapes, (LAYERS, PAIRS)]],
        in_specs=[pl.BlockSpec(memory_space=pltpu.HBM)] * 2 + [FAR] * len(earlier),
        out_specs=[WHOLE] * (len(pieces) + 1),
        scratch_shapes=[pltpu.SemaphoreType.DMA((len(pieces) + 1,))],
        name="pack",
        **limits(1000, 2**20),
    )(slab, angles, *earlier)


def inner_call(pairing, offsets, weights, slab, angles):
    return pl.pallas_call(
        inner_kernel,
        out_shape=(EVOLVED, STATES, ADJOINT, TABLE, jax.ShapeDtypeStruct((LAYERS, 512), jnp.float32)),
        in_specs=[SMALL, SMALL, SMALL, FAR, WHOLE],
        out_specs=(FAR, WHOLE, WHOLE, WHOLE, WHOLE),
        scratch_shapes=[
            room(2, ROWS + 8, 128),
            room(LAYERS - 1, 2, 2, 512 + 16, 128),
            room(LAYERS, 512 + 16, 128),
            room(2, ROWS + 16, 128),
            pltpu.SemaphoreType.DMA((4,)),
        ],
        name="inner",
        **limits(60_000_000, 24 * 2**20),
    )(pairing, offsets, weights, slab, angles)


def left_call(pairing, offsets, weights, slab, before, evolved, states, adjoint, table, inner):
    return pl.pallas_call(
        left_kernel,
        out_shape=(EVOLVED, STATES, ADJOINT, TABLE, HALO_TABLE, jax.ShapeDtypeStruct((LAYERS, 512), jnp.float32)),
        in_specs=[SMALL, SMALL, SMALL, FAR, WHOLE, FAR, WHOLE, WHOLE, WHOLE, WHOLE],
        out_specs=(FAR, WHOLE, WHOLE, WHOLE, WHOLE, WHOLE),
        scratch_shapes=[
            room(2, 328, 128),
            room(LAYERS, 2, 2, WINDOW + 16, 128),
            room(2, 2, 552, 128),
            room(LAYERS - 1, 2, 2, 160 + 16, 128),
            room(LAYERS, 280, 128),
            room(2, 40, 128),
            pltpu.SemaphoreType.DMA((6,)),
        ],
        input_output_aliases={5: 0, 6: 1, 7: 2, 8: 3},
        name="left",
        **limits(15_000_000, 8 * 2**20),
    )(pairing, offsets, weights, slab, before, evolved, states, adjoint, table, inner)


def left_far_call(pairing, offsets, weights, before, before_far, states, table, halo_table, rest, adjoint):
    return pl.pallas_call(
        left_far_kernel,
        out_shape=(ADJOINT, jax.ShapeDtypeStruct((LAYERS, PAIRS), jnp.float32)),
        in_specs=[SMALL, SMALL, SMALL] + [WHOLE] * 7,
        out_specs=(WHOLE, WHOLE),
        scratch_shapes=[
            room(2, 280, 128),
            room(LAYERS, 2, 2, FAR_WINDOW + 16, 128),
            room(2, 2, 408, 128),
            room(LAYERS - 1, 2, 2, 144 + 16, 128),
            room(LAYERS, 160, 128),
            pltpu.SemaphoreType.DMA((4,)),
        ],
        input_output_aliases={9: 0},
        name="left_far",
        **limits(10_000_000, 8 * 2**20),
    )(pairing, offsets, weights, before, before_far, states, table, halo_table, rest, adjoint)


def right_call(*operands):
    return pl.pallas_call(
        right_kernel,
        out_shape=(EVOLVED, STATES, ADJOINT, TABLE, jax.ShapeDtypeStruct((LAYERS, 896), jnp.float32)),
        in_specs=[SMALL, SMALL, SMALL, FAR] + [WHOLE] * 4 + [FAR, WHOLE, WHOLE, WHOLE],
        out_specs=(FAR, WHOLE, WHOLE, WHOLE, WHOLE),
        scratch_shapes=[
            room(2, 2 * FULL_WINDOW + 8, 128),
            room(LAYERS, 2, 2, FULL_WINDOW + 16, 128),
            room(2, 2, 560, 128),
            room(LAYERS - 1, 2, 2, 288 + 16, 128),
            room(LAYERS, 304, 128),
            room(2 * LAYERS, 304, 128),
            room(2, 40, 128),
            pltpu.SemaphoreType.DMA((8,)),
        ],
        input_output_aliases={8: 0, 9: 1, 10: 2, 11: 3},
        name="right",
        **limits(20_000_000, 8 * 2**20),
    )(*operands)


def on_device(slab, angles, pairing, band_offsets, band_weights):
    count = lax.axis_size("blk")
    onward = [(i, (i + 1) % count) for i in range(count)]
    back = [((i + 1) % count, i) for i in range(count)]
    tail, far_tail, head, far_head, angles_near = pack_call(
        slab, angles, ((ROWS - NEAR, NEAR, 512), (ROWS - NEAR - SENT, SENT, None), (0, NEAR, 0), (NEAR, SENT, None))
    )
    before = lax.ppermute(tail, "blk", onward)
    before_far = lax.ppermute(far_tail, "blk", onward)
    after = lax.ppermute(head, "blk", back)
    after_far = lax.ppermute(far_head, "blk", back)
    scalars = [pltpu.with_memory_space_constraint(x, pltpu.HBM) for x in (pairing, band_offsets, band_weights)]
    evolved, states, adjoint, table, inner = inner_call(*scalars, slab, angles_near)
    evolved, states, adjoint, table, left_table, left = left_call(
        *scalars, slab, before, evolved, states, adjoint, table, inner
    )
    evolved, states, adjoint, table, rest = right_call(
        *scalars, slab, after, after_far, inner, left, evolved, states, adjoint, table
    )
    _, gradient = left_far_call(*scalars, before, before_far, states, table, left_table, rest, adjoint)
    columns = lax.axis_size("col")
    step = 1
    while step < columns:
        gradient = gradient + lax.ppermute(gradient, "col", [(i, i ^ step) for i in range(columns)])
        step *= 2
    return (evolved, gradient)


def solution(mesh):
    in_specs = (P("blk", "col"), P(None, "blk"), P(), P(), P())
    out_specs = (P("blk", "col"), P(None, "blk"))
    return jax.shard_map(
        on_device, mesh=mesh, in_specs=in_specs, out_specs=out_specs, check_vma=False
    )
```

```python
import jax
import jax.numpy as jnp
from jax import lax
from jax.experimental import pallas as pl
from jax.experimental.pallas import tpu as pltpu
from jax.sharding import PartitionSpec as P

LAYERS = 4
REACH = 512
BANDS = 8
ROWS = 2048
PAIRS = 1024
NEAR = 280
FAR_ROWS = 240
HALO = NEAR + FAR_ROWS
SENT = 272
HEAD = 256
EARLY = 2
PAD = 272
LENGTH = PAD + PAIRS + PAD
WINDOW = 160
FAR_WINDOW = 136
RIGHT_WINDOW = 144
RIGHT_FAR_WINDOW = 152
FRONT = 8
GFRONT = 8


def fill_table(table, at, angle, low=0, high=128):
    both = jnp.concatenate([jnp.cos(angle), jnp.sin(angle)], 0)
    tall = jnp.transpose(both)
    for lane in range(2 * LAYERS):
        table[lane, pl.ds(at, high - low), :] = jnp.broadcast_to(tall[low:high, lane : lane + 1], (high - low, 128))


def forward(raw, states, start, table, table_start, lead, pairs, step):
    for layer in range(LAYERS):
        odd = layer % 2

        def block(i, carry, layer=layer, odd=odd):
            at = pl.multiple_of(i * step, 8)
            angle_at = at + table_start + lead if odd else at + table_start
            cosine = table[layer, pl.ds(angle_at, step), :]
            sine = table[LAYERS + layer, pl.ds(angle_at, step), :]
            for half in range(2):
                if layer == 0:
                    first = raw[half, pl.ds(2 * at + lead, step, stride=2), :]
                    second = raw[half, pl.ds(2 * at + lead + 1, step, stride=2), :]
                elif odd:
                    first = states[layer - 1, 1, half, pl.ds(at + start, step), :]
                    second = states[layer - 1, 0, half, pl.ds(at + start + 1, step), :]
                else:
                    first = states[layer - 1, 0, half, pl.ds(at + start - 1, step), :]
                    second = states[layer - 1, 1, half, pl.ds(at + start, step), :]
                states[layer, odd, half, pl.ds(at + start, step), :] = cosine * first - sine * second
                states[layer, 1 - odd, half, pl.ds(at + start, step), :] = sine * first + cosine * second
            return carry

        lax.fori_loop(0, pairs // step, block, 0)


def band(source, source_start, total, total_start, offsets, weights, pairs, step, signs, add):
    where = []
    for parity in range(2):
        for k in range(BANDS):
            for sign in signs:
                row = parity + sign * offsets[k]
                side = lax.bitwise_and(row, 1)
                where.append((side, lax.shift_right_arithmetic(row, 1) - 1 + side + source_start))

    def block(i, carry):
        at = pl.multiple_of(i * step, 8)
        for parity in range(2):
            for half in range(2):
                place = (parity, half, pl.ds(at + total_start, step), slice(None))
                value = total[place] if add else None
                for k in range(BANDS):
                    term = None
                    for n in range(len(signs)):
                        side, shift = where[(parity * BANDS + k) * len(signs) + n]
                        row = source[side, half, pl.ds(at + shift, step), :]
                        term = row if term is None else term + row
                    term = weights[k] * term
                    value = term if value is None else value + term
                total[place] = value
        return carry

    lax.fori_loop(0, pairs // step, block, 0)


def backward(states, start, adjoint, adjoint_start, turned, products, table, table_start, lead, pairs, step):
    for layer in reversed(range(LAYERS)):
        odd = layer % 2

        def block(i, carry, layer=layer, odd=odd):
            at = pl.multiple_of(i * step, 8)
            angle_at = at + table_start + lead if odd else at + table_start
            cosine = table[layer, pl.ds(angle_at, step), :]
            sine = table[LAYERS + layer, pl.ds(angle_at, step), :]
            product = None
            for half in range(2):
                source = adjoint if layer == LAYERS - 1 else turned.at[layer]
                begin = adjoint_start if layer == LAYERS - 1 else FRONT
                if odd:
                    first = source[1, half, pl.ds(at + begin, step), :]
                    second = source[0, half, pl.ds(at + begin + 1, step), :]
                else:
                    first = source[0, half, pl.ds(at + begin - 1, step), :]
                    second = source[1, half, pl.ds(at + begin, step), :]
                state_first = states[layer, odd, half, pl.ds(at + start, step), :]
                state_second = states[layer, 1 - odd, half, pl.ds(at + start, step), :]
                part = second * state_first - first * state_second
                product = part if product is None else product + part
                if layer:
                    turned[layer - 1, odd, half, pl.ds(at + FRONT, step), :] = cosine * first + sine * second
                    turned[layer - 1, 1 - odd, half, pl.ds(at + FRONT, step), :] = cosine * second - sine * first
            products[layer, pl.ds(at + GFRONT, step), :] = product
            return carry

        lax.fori_loop(0, pairs // step, block, 0)


def summed(products, lead, at):
    rows = []
    for layer in range(LAYERS):
        block = products[layer, pl.ds(at + GFRONT - lead if layer % 2 else at + GFRONT, 128), :]
        rows.append(jnp.sum(jnp.transpose(block), axis=0, keepdims=True))
    return jnp.concatenate(rows, 0)


def fetching(sources, scalars):
    copies = [pltpu.make_async_copy(source, scalars[n], scalars[3].at[n]) for n, source in enumerate(sources)]
    for copy in copies:
        copy.start()
    return copies


def fetched(sources, scalars):
    for copy in fetching(sources, scalars):
        copy.wait()
    return scalars[:3]


def evolve(pairing, slab, angles, states, table, raw, flags, sems):
    scalar = pltpu.make_async_copy(pairing, flags, sems.at[2])
    scalar.start()
    loads = []
    for half in range(2):
        loads.append(pltpu.make_async_copy(slab.at[:, pl.ds(128 * half, 128)], raw.at[half, pl.ds(0, ROWS), :], sems.at[half]))
        loads[-1].start()
    for tile in range(8):
        fill_table(table, FRONT + 128 * tile, angles[:, 128 * tile : 128 * (tile + 1)])
    for load in loads:
        load.wait()
    scalar.wait()
    forward(raw, states, PAD, table, FRONT, flags[0], PAIRS, 128)


def early_kernel(pairing, slab, angles, head_in, far_head_in, states, table, head, far_head, raw, flags, sems):
    @pl.when(lax.axis_index("blk") < EARLY)
    def _():
        evolve(pairing, slab, angles, states, table, raw, flags, sems)


def later_kernel(pairing, slab, angles, states_in, table_in, states, table, raw, flags, sems):
    @pl.when(lax.axis_index("blk") >= EARLY)
    def _():
        evolve(pairing, slab, angles, states, table, raw, flags, sems)


def inner_kernel(
    pairing, offsets, weights, states_in, table, evolved, states, adjoint, gradient, turned, products, out, sems, *scalars
):
    pairing, offsets, weights = fetched((pairing, offsets, weights), scalars)
    lead = pairing[0]

    def weave(i, carry):
        at = pl.multiple_of(i * 128, 128)
        for half in range(2):
            out[half, pl.ds(2 * at + lead + FRONT, 128, stride=2), :] = states[3, 0, half, pl.ds(at + PAD - 1, 128), :]
            out[half, pl.ds(2 * at + lead + FRONT + 1, 128, stride=2), :] = states[3, 1, half, pl.ds(at + PAD, 128), :]
        return carry

    lax.fori_loop(0, PAIRS // 128, weave, 0)
    stores = []
    for half in range(2):
        stores.append(
            pltpu.make_async_copy(out.at[half, pl.ds(FRONT, ROWS), :], evolved.at[:, pl.ds(128 * half, 128)], sems.at[half])
        )
        stores[-1].start()
    blank = jnp.zeros((PAD + 8, 128), jnp.float32)
    for parity in range(2):
        for half in range(2):
            states[LAYERS - 1, parity, half, pl.ds(0, PAD + 8), :] = blank
            states[LAYERS - 1, parity, half, pl.ds(PAD + PAIRS - 8, PAD + 8), :] = blank
    last = states.at[LAYERS - 1]
    band(last, PAD - 8, adjoint, FRONT, offsets, weights, PAIRS + 16, 104, (1, -1), False)
    backward(states, PAD + 256, adjoint, FRONT + 8 + 256, turned, products, table, FRONT + 256, lead, 512, 128)
    for tile in range(4):
        gradient[:, 128 * tile : 128 * (tile + 1)] = summed(products, lead, 128 * tile)
    for store in stores:
        store.wait()


def halo_angles(halo, at, tile):
    return halo[at + 4 * (tile // 2) : at + 4 * (tile // 2) + 4, 128 * (tile % 2) : 128 * (tile % 2) + 128]


def started(pieces, raw, sems):
    loads = []
    for half in range(2):
        for piece, piece_at, at, rows in pieces:
            load = pltpu.make_async_copy(
                piece.at[pl.ds(piece_at, rows), pl.ds(128 * half, 128)], raw.at[half, pl.ds(at, rows), :], sems.at[len(loads)]
            )
            load.start()
            loads.append(load)
    return loads


def near_tables(side, halo, at, table, halo_table):
    if side == 0:
        fill_table(halo_table, 0, halo_angles(halo, at, 1), 120, 128)
        fill_table(halo_table, 8, halo_angles(halo, at, 2))
        fill_table(halo_table, 136, halo_angles(halo, at, 3))
    else:
        fill_table(halo_table, 16, halo_angles(halo, at, 0))
        fill_table(halo_table, 144, halo_angles(halo, at, 1))
        fill_table(halo_table, 272, halo_angles(halo, at, 2), 0, 16)
    for lane in range(2 * LAYERS):
        if side == 0:
            halo_table[lane, pl.ds(264, 24), :] = table[lane, pl.ds(FRONT, 24), :]
            table[lane, pl.ds(0, FRONT), :] = halo_table[lane, pl.ds(256, 8), :]
        else:
            halo_table[lane, pl.ds(0, 16), :] = table[lane, pl.ds(FRONT + PAIRS - 16, 16), :]
            table[lane, pl.ds(FRONT + PAIRS, 16), :] = halo_table[lane, pl.ds(16, 16), :]


def boundary(side, at, lead, window, states, out, evolved, sems):
    stores = []
    for half in range(2):
        out[half, pl.ds(lead, 16, stride=2), :] = window[3, 0, half, pl.ds(at - 9, 16), :]
        out[half, pl.ds(lead + 1, 16, stride=2), :] = window[3, 1, half, pl.ds(at - 8, 16), :]
        store = pltpu.make_async_copy(
            out.at[half, pl.ds(16, 16), :],
            evolved.at[pl.ds((0, ROWS - 16)[side], 16), pl.ds(128 * half, 128)],
            sems.at[half],
        )
        store.start()
        stores.append(store)
        for parity in range(2):
            for layer in range(LAYERS):
                states[layer, parity, half, pl.ds(PAD + (-8, PAIRS - 8)[side], 16), :] = window[
                    layer, parity, half, pl.ds(at + (-8, 0)[side], 16), :
                ]
    return stores


def left_kernel(
    pairing, offsets, weights, slab, before, evolved_in, states_in, adjoint_in, table_in, inner,
    evolved, states, adjoint, table, halo_table, gradient, raw, window, source, turned, products, out, sems, *scalars,
):
    copies = fetching((pairing, offsets, weights), scalars)
    loads = started(((before, 0, 8, NEAR), (slab, 0, 8 + NEAR, 40)), raw, sems)
    near_tables(0, before, NEAR, table, halo_table)
    for load in loads + copies:
        load.wait()
    pairing, offsets, weights = scalars[:3]
    lead = pairing[0]
    forward(raw, window, FRONT, halo_table, 120, lead, WINDOW, 80)
    stores = boundary(0, FRONT + 144, lead, window, states, out, evolved, sems.at[pl.ds(4, 2)])
    blank = jnp.zeros((272, 128), jnp.float32)
    for half in range(2):
        for parity in range(2):
            source[parity, half, pl.ds(0, 136), :] = blank[:136]
            source[parity, half, pl.ds(136, 144), :] = window[3, parity, half, pl.ds(FRONT + 8, 144), :]
            source[parity, half, pl.ds(280, 272), :] = blank
    band(source, 264, adjoint, FRONT, offsets, weights, 288, 96, (-1,), True)
    band(source, 264, adjoint, FRONT, offsets, weights, 16, 16, (1,), True)
    backward(states, PAD + 120, adjoint, FRONT + 8 + 120, turned, products, table, FRONT + 120, lead, 160, 80)
    lane = lax.broadcasted_iota(jnp.int32, (LAYERS, 128), 1)
    gradient[:, 0:128] = summed(products, lead, 8)
    gradient[:, 128:256] = jnp.where(lane < 16, summed(products, lead, 136), inner[:, 0:128])
    gradient[:, 256:512] = inner[:, 128:384]
    for store in stores:
        store.wait()


def left_far_kernel(
    pairing, offsets, weights, before, before_far, states, table, halo_table, rest, adjoint_in,
    adjoint, gradient, raw, window, source, turned, products, sems, *scalars,
):
    copies = fetching((pairing, offsets, weights), scalars)
    loads = started(((before_far, SENT - FAR_ROWS, 8, FAR_ROWS), (before, 0, 8 + FAR_ROWS, 32)), raw, sems)
    blank = jnp.zeros((272, 128), jnp.float32)
    for half in range(2):
        for parity in range(2):
            source[parity, half, pl.ds(136, 272), :] = blank
    gradient[:, 128:896] = rest[...]
    for load in loads + copies:
        load.wait()
    pairing, offsets, weights = scalars[:3]
    lead = pairing[0]
    forward(raw, window, FRONT, halo_table, 0, lead, FAR_WINDOW, 136)
    for half in range(2):
        for parity in range(2):
            source[parity, half, pl.ds(8, 128), :] = window[3, parity, half, pl.ds(FRONT, 128), :]
    band(source, 264, adjoint, FRONT, offsets, weights, 144, 144, (-1,), True)
    backward(states, PAD - 8, adjoint, FRONT, turned, products, table, FRONT - 8, lead, 144, 144)
    gradient[:, 0:128] = summed(products, lead, 8)


def right_kernel(
    pairing, offsets, weights, slab, after, inner, left, evolved_in, states_in, adjoint_in, table_in,
    evolved, states, adjoint, table, halo_table, gradient, raw, window, source, turned, products, out, sems, *scalars,
):
    copies = fetching((pairing, offsets, weights), scalars)
    loads = started(((slab, ROWS - 32, 0, 32), (after, 0, 32, HEAD)), raw, sems)
    near_tables(1, after, HEAD, table, halo_table)
    blank = jnp.zeros((272, 128), jnp.float32)
    for half in range(2):
        for parity in range(2):
            source[parity, half, pl.ds(0, 272), :] = blank
            source[parity, half, pl.ds(400, 152), :] = blank[:152]
    gradient[:, 0:512] = left[...]
    for load in loads + copies:
        load.wait()
    pairing, offsets, weights = scalars[:3]
    lead = pairing[0]
    forward(raw, window, FRONT, halo_table, 0, lead, RIGHT_WINDOW, 72)
    stores = boundary(1, FRONT + 8, lead, window, states, out, evolved, sems.at[pl.ds(4, 2)])
    for half in range(2):
        for parity in range(2):
            source[parity, half, pl.ds(272, 128), :] = window[3, parity, half, pl.ds(FRONT + 8, 128), :]
    band(source, 0, adjoint, FRONT + 752, offsets, weights, 288, 144, (1,), True)
    band(source, 272, adjoint, FRONT + PAIRS, offsets, weights, 16, 16, (-1,), True)
    backward(states, PAD + 744, adjoint, FRONT + 8 + 744, turned, products, table, FRONT + 744, lead, 144, 144)
    lane = lax.broadcasted_iota(jnp.int32, (LAYERS, 128), 1)
    gradient[:, 512:640] = jnp.where(lane < 112, inner[:, 384:512], pltpu.roll(summed(products, lead, 8), 112, 1))
    gradient[:, 640:768] = summed(products, lead, 24)
    for store in stores:
        store.wait()


def right_far_kernel(
    pairing, offsets, weights, after, after_far, states, table, halo_table, rest, adjoint_in,
    adjoint, gradient, raw, window, source, turned, products, sems, *scalars,
):
    copies = fetching((pairing, offsets, weights), scalars)
    loads = started(((after, HEAD - 32, 0, 32), (after_far, 0, 32, HALO - HEAD)), raw, sems)
    blank = jnp.zeros((272, 128), jnp.float32)
    for half in range(2):
        for parity in range(2):
            source[parity, half, pl.ds(0, 272), :] = blank
    gradient[:, 0:768] = rest[:, 0:768]
    for load in loads + copies:
        load.wait()
    pairing, offsets, weights = scalars[:3]
    lead = pairing[0]
    forward(raw, window, FRONT, halo_table, 128, lead, RIGHT_FAR_WINDOW, 152)
    for half in range(2):
        for parity in range(2):
            source[parity, half, pl.ds(272, 144), :] = window[3, parity, half, pl.ds(FRONT + 8, 144), :]
    band(source, 0, adjoint, FRONT + 880, offsets, weights, 160, 160, (1,), True)
    backward(states, PAD + 872, adjoint, FRONT + 8 + 872, turned, products, table, FRONT + 872, lead, 160, 160)
    lane = lax.broadcasted_iota(jnp.int32, (LAYERS, 128), 1)
    gradient[:, 768:896] = jnp.where(lane < 112, rest[:, 768:896], pltpu.roll(summed(products, lead, 8), 112, 1))
    gradient[:, 896:1024] = summed(products, lead, 24)


WHOLE = pl.BlockSpec(memory_space=pltpu.VMEM)
FAR = pl.BlockSpec(memory_space=pl.ANY)

EVOLVED = jax.ShapeDtypeStruct((ROWS, 256), jnp.float32)
STATES = jax.ShapeDtypeStruct((LAYERS, 2, 2, LENGTH, 128), jnp.float32)
ADJOINT = jax.ShapeDtypeStruct((2, 2, PAIRS + 32, 128), jnp.float32)
TABLE = jax.ShapeDtypeStruct((2 * LAYERS, PAIRS + 32, 128), jnp.float32)
HALO_TABLE = jax.ShapeDtypeStruct((2 * LAYERS, 304, 128), jnp.float32)


def limits(flops, traffic, grant=16):
    return dict(
        compiler_params=pltpu.CompilerParams(vmem_limit_bytes=grant * 2**20),
        cost_estimate=pl.CostEstimate(flops=flops, bytes_accessed=traffic, transcendentals=8192),
    )


def room(*shape):
    return pltpu.VMEM(shape, jnp.float32)


def pack_call(slab, angles, pieces, *earlier):
    shapes = [(rows + (0 if lane is None else 8), 256) for _, rows, lane in pieces]

    def kernel(slab, angles, *refs):
        packed, tiles, sems = refs[len(earlier) : len(earlier) + len(pieces)], refs[-2], refs[-1]
        copies = [pltpu.make_async_copy(angles, tiles, sems.at[len(pieces)])]
        for n, (first, rows, _) in enumerate(pieces):
            copies.append(
                pltpu.make_async_copy(slab.at[pl.ds(first, rows), :], packed[n].at[pl.ds(0, rows), :], sems.at[n])
            )
        for copy in copies:
            copy.start()
        copies[0].wait()
        for n, (_, rows, lane) in enumerate(pieces):
            if lane is not None:
                for row in range(2):
                    lanes = slice(lane + 256 * row, lane + 256 * (row + 1))
                    packed[n][rows + 4 * row : rows + 4 * (row + 1), :] = tiles[:, lanes]
        for copy in copies[1:]:
            copy.wait()

    slab = pltpu.with_memory_space_constraint(slab, pltpu.HBM)
    angles = pltpu.with_memory_space_constraint(angles, pltpu.HBM)
    return pl.pallas_call(
        kernel,
        out_shape=[jax.ShapeDtypeStruct(shape, jnp.float32) for shape in [*shapes, (LAYERS, PAIRS)]],
        in_specs=[pl.BlockSpec(memory_space=pltpu.HBM)] * 2 + [FAR] * len(earlier),
        out_specs=[WHOLE] * (len(pieces) + 1),
        scratch_shapes=[pltpu.SemaphoreType.DMA((len(pieces) + 1,))],
        name="pack",
        **limits(1000, 2**20),
    )(slab, angles, *earlier)


SCALARS = [
    pltpu.SMEM((LAYERS,), jnp.int32),
    pltpu.SMEM((BANDS,), jnp.int32),
    pltpu.SMEM((BANDS,), jnp.float32),
    pltpu.SemaphoreType.DMA((3,)),
]
EVOLVE_ROOM = [room(2, ROWS + 8, 128), pltpu.SMEM((LAYERS,), jnp.int32), pltpu.SemaphoreType.DMA((3,))]


def early_call(pairing, slab, angles, head, far_head):
    return pl.pallas_call(
        early_kernel,
        out_shape=(STATES, TABLE) + tuple(jax.ShapeDtypeStruct(x.shape, x.dtype) for x in (head, far_head)),
        in_specs=[FAR, FAR, WHOLE, FAR, FAR],
        out_specs=(WHOLE, WHOLE, FAR, FAR),
        scratch_shapes=EVOLVE_ROOM,
        input_output_aliases={3: 2, 4: 3},
        name="early",
        **limits(12_000_000, 8 * 2**20),
    )(pairing, slab, angles, head, far_head)


def later_call(pairing, slab, angles, states, table):
    return pl.pallas_call(
        later_kernel,
        out_shape=(STATES, TABLE),
        in_specs=[FAR, FAR, WHOLE, WHOLE, WHOLE],
        out_specs=(WHOLE, WHOLE),
        scratch_shapes=EVOLVE_ROOM,
        input_output_aliases={3: 0, 4: 1},
        name="later",
        **limits(12_000_000, 8 * 2**20),
    )(pairing, slab, angles, states, table)


def inner_call(pairing, offsets, weights, states, table):
    return pl.pallas_call(
        inner_kernel,
        out_shape=(EVOLVED, STATES, ADJOINT, jax.ShapeDtypeStruct((LAYERS, 512), jnp.float32)),
        in_specs=[FAR, FAR, FAR, WHOLE, WHOLE],
        out_specs=(FAR, WHOLE, WHOLE, WHOLE),
        scratch_shapes=[
            room(LAYERS - 1, 2, 2, 512 + 16, 128),
            room(LAYERS, 512 + 16, 128),
            room(2, ROWS + 16, 128),
            pltpu.SemaphoreType.DMA((2,)),
            *SCALARS,
        ],
        input_output_aliases={3: 1},
        name="inner",
        **limits(50_000_000, 16 * 2**20),
    )(pairing, offsets, weights, states, table)


def left_call(pairing, offsets, weights, slab, before, evolved, states, adjoint, table, inner):
    return pl.pallas_call(
        left_kernel,
        out_shape=(EVOLVED, STATES, ADJOINT, TABLE, HALO_TABLE, jax.ShapeDtypeStruct((LAYERS, 512), jnp.float32)),
        in_specs=[FAR, FAR, FAR, FAR, WHOLE, FAR, WHOLE, WHOLE, WHOLE, WHOLE],
        out_specs=(FAR, WHOLE, WHOLE, WHOLE, WHOLE, WHOLE),
        scratch_shapes=[
            room(2, 328, 128),
            room(LAYERS, 2, 2, WINDOW + 16, 128),
            room(2, 2, 552, 128),
            room(LAYERS - 1, 2, 2, 160 + 16, 128),
            room(LAYERS, 280, 128),
            room(2, 40, 128),
            pltpu.SemaphoreType.DMA((6,)),
            *SCALARS,
        ],
        input_output_aliases={5: 0, 6: 1, 7: 2, 8: 3},
        name="left",
        **limits(15_000_000, 8 * 2**20),
    )(pairing, offsets, weights, slab, before, evolved, states, adjoint, table, inner)


def left_far_call(pairing, offsets, weights, before, before_far, states, table, halo_table, rest, adjoint):
    return pl.pallas_call(
        left_far_kernel,
        out_shape=(ADJOINT, jax.ShapeDtypeStruct((LAYERS, 896), jnp.float32)),
        in_specs=[FAR, FAR, FAR] + [WHOLE] * 7,
        out_specs=(WHOLE, WHOLE),
        scratch_shapes=[
            room(2, 280, 128),
            room(LAYERS, 2, 2, FAR_WINDOW + 16, 128),
            room(2, 2, 408, 128),
            room(LAYERS - 1, 2, 2, 144 + 16, 128),
            room(LAYERS, 160, 128),
            pltpu.SemaphoreType.DMA((4,)),
            *SCALARS,
        ],
        input_output_aliases={9: 0},
        name="left_far",
        **limits(10_000_000, 8 * 2**20),
    )(pairing, offsets, weights, before, before_far, states, table, halo_table, rest, adjoint)


def right_call(*operands):
    return pl.pallas_call(
        right_kernel,
        out_shape=(EVOLVED, STATES, ADJOINT, TABLE, HALO_TABLE, jax.ShapeDtypeStruct((LAYERS, 768), jnp.float32)),
        in_specs=[FAR, FAR, FAR, FAR] + [WHOLE] * 3 + [FAR, WHOLE, WHOLE, WHOLE],
        out_specs=(FAR, WHOLE, WHOLE, WHOLE, WHOLE, WHOLE),
        scratch_shapes=[
            room(2, 2 * RIGHT_WINDOW + 8, 128),
            room(LAYERS, 2, 2, RIGHT_WINDOW + 16, 128),
            room(2, 2, 560, 128),
            room(LAYERS - 1, 2, 2, 144 + 16, 128),
            room(LAYERS, 168, 128),
            room(2, 40, 128),
            pltpu.SemaphoreType.DMA((6,)),
            *SCALARS,
        ],
        input_output_aliases={7: 0, 8: 1, 9: 2, 10: 3},
        name="right",
        **limits(15_000_000, 8 * 2**20),
    )(*operands)


def right_far_call(*operands):
    return pl.pallas_call(
        right_far_kernel,
        out_shape=(ADJOINT, jax.ShapeDtypeStruct((LAYERS, PAIRS), jnp.float32)),
        in_specs=[FAR, FAR, FAR] + [WHOLE] * 7,
        out_specs=(WHOLE, WHOLE),
        scratch_shapes=[
            room(2, 2 * RIGHT_FAR_WINDOW + 8, 128),
            room(LAYERS, 2, 2, RIGHT_FAR_WINDOW + 16, 128),
            room(2, 2, 440, 128),
            room(LAYERS - 1, 2, 2, 160 + 16, 128),
            room(LAYERS, 176, 128),
            pltpu.SemaphoreType.DMA((4,)),
            *SCALARS,
        ],
        input_output_aliases={9: 0},
        name="right_far",
        **limits(10_000_000, 8 * 2**20),
    )(*operands)


def on_device(slab, angles, pairing, band_offsets, band_weights):
    count = lax.axis_size("blk")
    onward = [(i, (i + 1) % count) for i in range(count)]
    back = [((i + 1) % count, i) for i in range(count)]
    tail, far_tail, head, far_head, angles_near = pack_call(
        slab, angles, ((ROWS - NEAR, NEAR, 512), (ROWS - NEAR - SENT, SENT, None), (0, HEAD, 0), (HEAD, HALO - HEAD, None))
    )
    before = lax.ppermute(tail, "blk", onward)
    before_far = lax.ppermute(far_tail, "blk", onward)
    scalars = [pltpu.with_memory_space_constraint(x, pltpu.HBM) for x in (pairing, band_offsets, band_weights)]
    states, table, head, far_head = early_call(scalars[0], slab, angles_near, head, far_head)
    after = lax.ppermute(head, "blk", back)
    after_far = lax.ppermute(far_head, "blk", back)
    states, table = later_call(scalars[0], slab, angles_near, states, table)
    evolved, states, adjoint, inner = inner_call(*scalars, states, table)
    evolved, states, adjoint, table, left_table, left = left_call(
        *scalars, slab, before, evolved, states, adjoint, table, inner
    )
    evolved, states, adjoint, table, right_table, rest = right_call(
        *scalars, slab, after, inner, left, evolved, states, adjoint, table
    )
    adjoint, rest = left_far_call(*scalars, before, before_far, states, table, left_table, rest, adjoint)
    _, gradient = right_far_call(*scalars, after, after_far, states, table, right_table, rest, adjoint)
    columns = lax.axis_size("col")
    step = 1
    while step < columns:
        gradient = gradient + lax.ppermute(gradient, "col", [(i, i ^ step) for i in range(columns)])
        step *= 2
    return (evolved, gradient)


def solution(mesh):
    in_specs = (P("blk", "col"), P(None, "blk"), P(), P(), P())
    out_specs = (P("blk", "col"), P(None, "blk"))
    return jax.shard_map(
        on_device, mesh=mesh, in_specs=in_specs, out_specs=out_specs, check_vma=False
    )
```

```python
import jax
import jax.numpy as jnp
from jax import lax
from jax.experimental import pallas as pl
from jax.experimental.pallas import tpu as pltpu
from jax.sharding import PartitionSpec as P

LAYERS = 4
REACH = 512
BANDS = 8
ROWS = 2048
PAIRS = 1024
NEAR = 280
FAR_ROWS = 240
HALO = NEAR + FAR_ROWS
SENT = 272
HEAD = 256
EARLY = 2
PAD = 272
LENGTH = PAD + PAIRS + PAD
WINDOW = 160
FAR_WINDOW = 136
RIGHT_WINDOW = 144
RIGHT_FAR_WINDOW = 152
FRONT = 8
GFRONT = 8


def fill_table(table, at, angle, low=0, high=128):
    both = jnp.concatenate([jnp.cos(angle), jnp.sin(angle)], 0)
    tall = jnp.transpose(both)
    for lane in range(2 * LAYERS):
        table[lane, pl.ds(at, high - low), :] = jnp.broadcast_to(tall[low:high, lane : lane + 1], (high - low, 128))


def forward(raw, states, start, table, table_start, lead, pairs, step):
    for layer in range(LAYERS):
        odd = layer % 2

        def block(i, carry, layer=layer, odd=odd):
            at = pl.multiple_of(i * step, 8)
            angle_at = at + table_start + lead if odd else at + table_start
            cosine = table[layer, pl.ds(angle_at, step), :]
            sine = table[LAYERS + layer, pl.ds(angle_at, step), :]
            for half in range(2):
                if layer == 0:
                    first = raw[half, pl.ds(2 * at + lead, step, stride=2), :]
                    second = raw[half, pl.ds(2 * at + lead + 1, step, stride=2), :]
                elif odd:
                    first = states[layer - 1, 1, half, pl.ds(at + start, step), :]
                    second = states[layer - 1, 0, half, pl.ds(at + start + 1, step), :]
                else:
                    first = states[layer - 1, 0, half, pl.ds(at + start - 1, step), :]
                    second = states[layer - 1, 1, half, pl.ds(at + start, step), :]
                states[layer, odd, half, pl.ds(at + start, step), :] = cosine * first - sine * second
                states[layer, 1 - odd, half, pl.ds(at + start, step), :] = sine * first + cosine * second
            return carry

        lax.fori_loop(0, pairs // step, block, 0)


def band(source, source_start, total, total_start, offsets, weights, pairs, step, signs, add):
    where = []
    for parity in range(2):
        for k in range(BANDS):
            for sign in signs:
                row = parity + sign * offsets[k]
                side = lax.bitwise_and(row, 1)
                where.append((side, lax.shift_right_arithmetic(row, 1) - 1 + side + source_start))

    def block(i, carry):
        at = pl.multiple_of(i * step, 8)
        for parity in range(2):
            for half in range(2):
                place = (parity, half, pl.ds(at + total_start, step), slice(None))
                value = total[place] if add else None
                for k in range(BANDS):
                    term = None
                    for n in range(len(signs)):
                        side, shift = where[(parity * BANDS + k) * len(signs) + n]
                        row = source[side, half, pl.ds(at + shift, step), :]
                        term = row if term is None else term + row
                    term = weights[k] * term
                    value = term if value is None else value + term
                total[place] = value
        return carry

    lax.fori_loop(0, pairs // step, block, 0)


def backward(states, start, adjoint, adjoint_start, turned, products, table, table_start, lead, pairs, step):
    for layer in reversed(range(LAYERS)):
        odd = layer % 2

        def block(i, carry, layer=layer, odd=odd):
            at = pl.multiple_of(i * step, 8)
            angle_at = at + table_start + lead if odd else at + table_start
            cosine = table[layer, pl.ds(angle_at, step), :]
            sine = table[LAYERS + layer, pl.ds(angle_at, step), :]
            product = None
            for half in range(2):
                source = adjoint if layer == LAYERS - 1 else turned.at[layer]
                begin = adjoint_start if layer == LAYERS - 1 else FRONT
                if odd:
                    first = source[1, half, pl.ds(at + begin, step), :]
                    second = source[0, half, pl.ds(at + begin + 1, step), :]
                else:
                    first = source[0, half, pl.ds(at + begin - 1, step), :]
                    second = source[1, half, pl.ds(at + begin, step), :]
                state_first = states[layer, odd, half, pl.ds(at + start, step), :]
                state_second = states[layer, 1 - odd, half, pl.ds(at + start, step), :]
                part = second * state_first - first * state_second
                product = part if product is None else product + part
                if layer:
                    turned[layer - 1, odd, half, pl.ds(at + FRONT, step), :] = cosine * first + sine * second
                    turned[layer - 1, 1 - odd, half, pl.ds(at + FRONT, step), :] = cosine * second - sine * first
            products[layer, pl.ds(at + GFRONT, step), :] = product
            return carry

        lax.fori_loop(0, pairs // step, block, 0)


def summed(products, lead, at):
    rows = []
    for layer in range(LAYERS):
        block = products[layer, pl.ds(at + GFRONT - lead if layer % 2 else at + GFRONT, 128), :]
        rows.append(jnp.sum(jnp.transpose(block), axis=0, keepdims=True))
    return jnp.concatenate(rows, 0)


def fetching(sources, scalars):
    copies = [pltpu.make_async_copy(source, scalars[n], scalars[3].at[n]) for n, source in enumerate(sources)]
    for copy in copies:
        copy.start()
    return copies


def fetched(sources, scalars):
    for copy in fetching(sources, scalars):
        copy.wait()
    return scalars[:3]


def evolve(pairing, slab, angles, states, table, raw, flags, sems):
    scalar = pltpu.make_async_copy(pairing, flags, sems.at[2])
    scalar.start()
    loads = []
    for half in range(2):
        loads.append(pltpu.make_async_copy(slab.at[:, pl.ds(128 * half, 128)], raw.at[half, pl.ds(0, ROWS), :], sems.at[half]))
        loads[-1].start()
    for tile in range(8):
        fill_table(table, FRONT + 128 * tile, angles[:, 128 * tile : 128 * (tile + 1)])
    for load in loads:
        load.wait()
    scalar.wait()
    forward(raw, states, PAD, table, FRONT, flags[0], PAIRS, 128)


def early_kernel(pairing, slab, angles, head_in, far_head_in, states, table, head, far_head, raw, flags, sems):
    @pl.when(lax.axis_index("blk") < EARLY)
    def _():
        evolve(pairing, slab, angles, states, table, raw, flags, sems)


def later_kernel(pairing, slab, angles, states_in, table_in, states, table, raw, flags, sems):
    @pl.when(lax.axis_index("blk") >= EARLY)
    def _():
        evolve(pairing, slab, angles, states, table, raw, flags, sems)


def inner_kernel(
    pairing, offsets, weights, states_in, table, evolved, states, adjoint, gradient, turned, products, out, sems, *scalars
):
    pairing, offsets, weights = fetched((pairing, offsets, weights), scalars)
    lead = pairing[0]

    def weave(i, carry):
        at = pl.multiple_of(i * 128, 128)
        for half in range(2):
            out[half, pl.ds(2 * at + lead + FRONT, 128, stride=2), :] = states[3, 0, half, pl.ds(at + PAD - 1, 128), :]
            out[half, pl.ds(2 * at + lead + FRONT + 1, 128, stride=2), :] = states[3, 1, half, pl.ds(at + PAD, 128), :]
        return carry

    lax.fori_loop(0, PAIRS // 128, weave, 0)
    stores = []
    for half in range(2):
        stores.append(
            pltpu.make_async_copy(out.at[half, pl.ds(FRONT, ROWS), :], evolved.at[:, pl.ds(128 * half, 128)], sems.at[half])
        )
        stores[-1].start()
    blank = jnp.zeros((PAD + 8, 128), jnp.float32)
    for parity in range(2):
        for half in range(2):
            states[LAYERS - 1, parity, half, pl.ds(0, PAD + 8), :] = blank
            states[LAYERS - 1, parity, half, pl.ds(PAD + PAIRS - 8, PAD + 8), :] = blank
    last = states.at[LAYERS - 1]
    band(last, PAD - 8, adjoint, FRONT, offsets, weights, PAIRS + 16, 104, (1, -1), False)
    backward(states, PAD + 256, adjoint, FRONT + 8 + 256, turned, products, table, FRONT + 256, lead, 512, 128)
    for tile in range(4):
        gradient[:, 128 * tile : 128 * (tile + 1)] = summed(products, lead, 128 * tile)
    for store in stores:
        store.wait()


def halo_angles(halo, at, tile):
    return halo[at + 4 * (tile // 2) : at + 4 * (tile // 2) + 4, 128 * (tile % 2) : 128 * (tile % 2) + 128]


def placed(pieces, raw):
    for piece, piece_at, at, rows in pieces:
        for half in range(2):
            raw[half, pl.ds(at, rows), :] = piece[pl.ds(piece_at, rows), 128 * half : 128 * half + 128]


def started(pieces, raw, sems):
    loads = []
    for half in range(2):
        for piece, piece_at, at, rows in pieces:
            load = pltpu.make_async_copy(
                piece.at[pl.ds(piece_at, rows), pl.ds(128 * half, 128)], raw.at[half, pl.ds(at, rows), :], sems.at[len(loads)]
            )
            load.start()
            loads.append(load)
    return loads


def near_tables(side, halo, at, table, halo_table):
    if side == 0:
        fill_table(halo_table, 0, halo_angles(halo, at, 1), 120, 128)
        fill_table(halo_table, 8, halo_angles(halo, at, 2))
        fill_table(halo_table, 136, halo_angles(halo, at, 3))
    else:
        fill_table(halo_table, 16, halo_angles(halo, at, 0))
        fill_table(halo_table, 144, halo_angles(halo, at, 1))
        fill_table(halo_table, 272, halo_angles(halo, at, 2), 0, 16)
    for lane in range(2 * LAYERS):
        if side == 0:
            halo_table[lane, pl.ds(264, 24), :] = table[lane, pl.ds(FRONT, 24), :]
            table[lane, pl.ds(0, FRONT), :] = halo_table[lane, pl.ds(256, 8), :]
        else:
            halo_table[lane, pl.ds(0, 16), :] = table[lane, pl.ds(FRONT + PAIRS - 16, 16), :]
            table[lane, pl.ds(FRONT + PAIRS, 16), :] = halo_table[lane, pl.ds(16, 16), :]


def boundary(side, at, lead, window, states, out, evolved, sems):
    stores = []
    for half in range(2):
        out[half, pl.ds(lead, 16, stride=2), :] = window[3, 0, half, pl.ds(at - 9, 16), :]
        out[half, pl.ds(lead + 1, 16, stride=2), :] = window[3, 1, half, pl.ds(at - 8, 16), :]
        store = pltpu.make_async_copy(
            out.at[half, pl.ds(16, 16), :],
            evolved.at[pl.ds((0, ROWS - 16)[side], 16), pl.ds(128 * half, 128)],
            sems.at[half],
        )
        store.start()
        stores.append(store)
        for parity in range(2):
            for layer in range(LAYERS):
                states[layer, parity, half, pl.ds(PAD + (-8, PAIRS - 8)[side], 16), :] = window[
                    layer, parity, half, pl.ds(at + (-8, 0)[side], 16), :
                ]
    return stores


def left_kernel(
    pairing, offsets, weights, slab, before, evolved_in, states_in, adjoint_in, table_in, inner,
    evolved, states, adjoint, table, halo_table, gradient, raw, window, source, turned, products, out, sems, *scalars,
):
    copies = fetching((pairing, offsets, weights), scalars)
    loads = started(((slab, 0, 8 + NEAR, 40),), raw, sems)
    placed(((before, 0, 8, NEAR),), raw)
    near_tables(0, before, NEAR, table, halo_table)
    for load in loads + copies:
        load.wait()
    pairing, offsets, weights = scalars[:3]
    lead = pairing[0]
    forward(raw, window, FRONT, halo_table, 120, lead, WINDOW, 80)
    stores = boundary(0, FRONT + 144, lead, window, states, out, evolved, sems.at[pl.ds(4, 2)])
    blank = jnp.zeros((272, 128), jnp.float32)
    for half in range(2):
        for parity in range(2):
            source[parity, half, pl.ds(0, 136), :] = blank[:136]
            source[parity, half, pl.ds(136, 144), :] = window[3, parity, half, pl.ds(FRONT + 8, 144), :]
            source[parity, half, pl.ds(280, 272), :] = blank
    band(source, 264, adjoint, FRONT, offsets, weights, 288, 96, (-1,), True)
    band(source, 264, adjoint, FRONT, offsets, weights, 16, 16, (1,), True)
    backward(states, PAD + 120, adjoint, FRONT + 8 + 120, turned, products, table, FRONT + 120, lead, 160, 80)
    lane = lax.broadcasted_iota(jnp.int32, (LAYERS, 128), 1)
    gradient[:, 0:128] = summed(products, lead, 8)
    gradient[:, 128:256] = jnp.where(lane < 16, summed(products, lead, 136), inner[:, 0:128])
    gradient[:, 256:512] = inner[:, 128:384]
    for store in stores:
        store.wait()


def left_far_kernel(
    pairing, offsets, weights, before, before_far, states, table, halo_table, rest, adjoint_in,
    adjoint, gradient, raw, window, source, turned, products, *scalars,
):
    copies = fetching((pairing, offsets, weights), scalars)
    placed(((before_far, SENT - FAR_ROWS, 8, FAR_ROWS), (before, 0, 8 + FAR_ROWS, 32)), raw)
    blank = jnp.zeros((272, 128), jnp.float32)
    for half in range(2):
        for parity in range(2):
            source[parity, half, pl.ds(136, 272), :] = blank
    gradient[:, 128:896] = rest[...]
    for load in copies:
        load.wait()
    pairing, offsets, weights = scalars[:3]
    lead = pairing[0]
    forward(raw, window, FRONT, halo_table, 0, lead, FAR_WINDOW, 136)
    for half in range(2):
        for parity in range(2):
            source[parity, half, pl.ds(8, 128), :] = window[3, parity, half, pl.ds(FRONT, 128), :]
    band(source, 264, adjoint, FRONT, offsets, weights, 144, 144, (-1,), True)
    backward(states, PAD - 8, adjoint, FRONT, turned, products, table, FRONT - 8, lead, 144, 144)
    gradient[:, 0:128] = summed(products, lead, 8)


def right_kernel(
    pairing, offsets, weights, slab, after, inner, left, evolved_in, states_in, adjoint_in, table_in,
    evolved, states, adjoint, table, halo_table, gradient, raw, window, source, turned, products, out, sems, *scalars,
):
    copies = fetching((pairing, offsets, weights), scalars)
    loads = started(((slab, ROWS - 32, 0, 32),), raw, sems)
    placed(((after, 0, 32, HEAD),), raw)
    near_tables(1, after, HEAD, table, halo_table)
    blank = jnp.zeros((272, 128), jnp.float32)
    for half in range(2):
        for parity in range(2):
            source[parity, half, pl.ds(0, 272), :] = blank
            source[parity, half, pl.ds(400, 152), :] = blank[:152]
    gradient[:, 0:512] = left[...]
    for load in loads + copies:
        load.wait()
    pairing, offsets, weights = scalars[:3]
    lead = pairing[0]
    forward(raw, window, FRONT, halo_table, 0, lead, RIGHT_WINDOW, 72)
    stores = boundary(1, FRONT + 8, lead, window, states, out, evolved, sems.at[pl.ds(4, 2)])
    for half in range(2):
        for parity in range(2):
            source[parity, half, pl.ds(272, 128), :] = window[3, parity, half, pl.ds(FRONT + 8, 128), :]
    band(source, 0, adjoint, FRONT + 752, offsets, weights, 288, 144, (1,), True)
    band(source, 272, adjoint, FRONT + PAIRS, offsets, weights, 16, 16, (-1,), True)
    backward(states, PAD + 744, adjoint, FRONT + 8 + 744, turned, products, table, FRONT + 744, lead, 144, 144)
    lane = lax.broadcasted_iota(jnp.int32, (LAYERS, 128), 1)
    gradient[:, 512:640] = jnp.where(lane < 112, inner[:, 384:512], pltpu.roll(summed(products, lead, 8), 112, 1))
    gradient[:, 640:768] = summed(products, lead, 24)
    for store in stores:
        store.wait()


def right_far_kernel(
    pairing, offsets, weights, after, after_far, states, table, halo_table, rest, adjoint_in,
    adjoint, gradient, raw, window, source, turned, products, *scalars,
):
    copies = fetching((pairing, offsets, weights), scalars)
    placed(((after, HEAD - 32, 0, 32), (after_far, 0, 32, HALO - HEAD)), raw)
    blank = jnp.zeros((272, 128), jnp.float32)
    for half in range(2):
        for parity in range(2):
            source[parity, half, pl.ds(0, 272), :] = blank
    gradient[:, 0:768] = rest[:, 0:768]
    for load in copies:
        load.wait()
    pairing, offsets, weights = scalars[:3]
    lead = pairing[0]
    forward(raw, window, FRONT, halo_table, 128, lead, RIGHT_FAR_WINDOW, 152)
    for half in range(2):
        for parity in range(2):
            source[parity, half, pl.ds(272, 144), :] = window[3, parity, half, pl.ds(FRONT + 8, 144), :]
    band(source, 0, adjoint, FRONT + 880, offsets, weights, 160, 160, (1,), True)
    backward(states, PAD + 872, adjoint, FRONT + 8 + 872, turned, products, table, FRONT + 872, lead, 160, 160)
    lane = lax.broadcasted_iota(jnp.int32, (LAYERS, 128), 1)
    gradient[:, 768:896] = jnp.where(lane < 112, rest[:, 768:896], pltpu.roll(summed(products, lead, 8), 112, 1))
    gradient[:, 896:1024] = summed(products, lead, 24)


WHOLE = pl.BlockSpec(memory_space=pltpu.VMEM)
FAR = pl.BlockSpec(memory_space=pl.ANY)

EVOLVED = jax.ShapeDtypeStruct((ROWS, 256), jnp.float32)
STATES = jax.ShapeDtypeStruct((LAYERS, 2, 2, LENGTH, 128), jnp.float32)
ADJOINT = jax.ShapeDtypeStruct((2, 2, PAIRS + 32, 128), jnp.float32)
TABLE = jax.ShapeDtypeStruct((2 * LAYERS, PAIRS + 32, 128), jnp.float32)
HALO_TABLE = jax.ShapeDtypeStruct((2 * LAYERS, 304, 128), jnp.float32)


def limits(flops, traffic, grant=16):
    return dict(
        compiler_params=pltpu.CompilerParams(vmem_limit_bytes=grant * 2**20),
        cost_estimate=pl.CostEstimate(flops=flops, bytes_accessed=traffic, transcendentals=8192),
    )


def room(*shape):
    return pltpu.VMEM(shape, jnp.float32)


def pack_call(slab, angles, pieces, *scalars):
    shapes = [(rows + (0 if lane is None else 8), 256) for _, rows, lane in pieces]

    def kernel(slab, angles, *refs):
        count = len(scalars)
        sources, packed, kept = refs[:count], refs[count : count + len(pieces)], refs[count + len(pieces) : -2]
        tiles, sems = refs[-2], refs[-1]
        copies = [pltpu.make_async_copy(angles, tiles, sems.at[len(pieces)])]
        for n, source in enumerate(sources):
            copies.append(pltpu.make_async_copy(source, kept[n], sems.at[len(pieces) + 1 + n]))
        for n, (first, rows, _) in enumerate(pieces):
            copies.append(
                pltpu.make_async_copy(slab.at[pl.ds(first, rows), :], packed[n].at[pl.ds(0, rows), :], sems.at[n])
            )
        for copy in copies:
            copy.start()
        copies[0].wait()
        for n, (_, rows, lane) in enumerate(pieces):
            if lane is not None:
                for row in range(2):
                    lanes = slice(lane + 256 * row, lane + 256 * (row + 1))
                    packed[n][rows + 4 * row : rows + 4 * (row + 1), :] = tiles[:, lanes]
        for copy in copies[1:]:
            copy.wait()

    slab = pltpu.with_memory_space_constraint(slab, pltpu.HBM)
    angles = pltpu.with_memory_space_constraint(angles, pltpu.HBM)
    return pl.pallas_call(
        kernel,
        out_shape=[jax.ShapeDtypeStruct(shape, jnp.float32) for shape in shapes]
        + [jax.ShapeDtypeStruct(x.shape, x.dtype) for x in (*scalars, angles)],
        in_specs=[pl.BlockSpec(memory_space=pltpu.HBM)] * (2 + len(scalars)),
        out_specs=[WHOLE] * (len(pieces) + len(scalars) + 1),
        scratch_shapes=[pltpu.SemaphoreType.DMA((len(pieces) + len(scalars) + 1,))],
        name="pack",
        **limits(1000, 2**20),
    )(slab, angles, *scalars)


SCALARS = [
    pltpu.SMEM((LAYERS,), jnp.int32),
    pltpu.SMEM((BANDS,), jnp.int32),
    pltpu.SMEM((BANDS,), jnp.float32),
    pltpu.SemaphoreType.DMA((3,)),
]
EVOLVE_ROOM = [room(2, ROWS + 8, 128), pltpu.SMEM((LAYERS,), jnp.int32), pltpu.SemaphoreType.DMA((3,))]


def early_call(pairing, slab, angles, head, far_head):
    return pl.pallas_call(
        early_kernel,
        out_shape=(STATES, TABLE) + tuple(jax.ShapeDtypeStruct(x.shape, x.dtype) for x in (head, far_head)),
        in_specs=[WHOLE, FAR, WHOLE, FAR, FAR],
        out_specs=(WHOLE, WHOLE, FAR, FAR),
        scratch_shapes=EVOLVE_ROOM,
        input_output_aliases={3: 2, 4: 3},
        name="early",
        **limits(12_000_000, 8 * 2**20),
    )(pairing, slab, angles, head, far_head)


def later_call(pairing, slab, angles, states, table):
    return pl.pallas_call(
        later_kernel,
        out_shape=(STATES, TABLE),
        in_specs=[WHOLE, FAR, WHOLE, WHOLE, WHOLE],
        out_specs=(WHOLE, WHOLE),
        scratch_shapes=EVOLVE_ROOM,
        input_output_aliases={3: 0, 4: 1},
        name="later",
        **limits(12_000_000, 8 * 2**20),
    )(pairing, slab, angles, states, table)


def inner_call(pairing, offsets, weights, states, table):
    return pl.pallas_call(
        inner_kernel,
        out_shape=(EVOLVED, STATES, ADJOINT, jax.ShapeDtypeStruct((LAYERS, 512), jnp.float32)),
        in_specs=[WHOLE, WHOLE, WHOLE, WHOLE, WHOLE],
        out_specs=(FAR, WHOLE, WHOLE, WHOLE),
        scratch_shapes=[
            room(LAYERS - 1, 2, 2, 512 + 16, 128),
            room(LAYERS, 512 + 16, 128),
            room(2, ROWS + 16, 128),
            pltpu.SemaphoreType.DMA((2,)),
            *SCALARS,
        ],
        input_output_aliases={3: 1},
        name="inner",
        **limits(50_000_000, 16 * 2**20),
    )(pairing, offsets, weights, states, table)


def left_call(pairing, offsets, weights, slab, before, evolved, states, adjoint, table, inner):
    return pl.pallas_call(
        left_kernel,
        out_shape=(EVOLVED, STATES, ADJOINT, TABLE, HALO_TABLE, jax.ShapeDtypeStruct((LAYERS, 512), jnp.float32)),
        in_specs=[WHOLE, WHOLE, WHOLE, FAR, WHOLE, FAR, WHOLE, WHOLE, WHOLE, WHOLE],
        out_specs=(FAR, WHOLE, WHOLE, WHOLE, WHOLE, WHOLE),
        scratch_shapes=[
            room(2, 328, 128),
            room(LAYERS, 2, 2, WINDOW + 16, 128),
            room(2, 2, 552, 128),
            room(LAYERS - 1, 2, 2, 160 + 16, 128),
            room(LAYERS, 280, 128),
            room(2, 40, 128),
            pltpu.SemaphoreType.DMA((6,)),
            *SCALARS,
        ],
        input_output_aliases={5: 0, 6: 1, 7: 2, 8: 3},
        name="left",
        **limits(15_000_000, 8 * 2**20),
    )(pairing, offsets, weights, slab, before, evolved, states, adjoint, table, inner)


def left_far_call(pairing, offsets, weights, before, before_far, states, table, halo_table, rest, adjoint):
    return pl.pallas_call(
        left_far_kernel,
        out_shape=(ADJOINT, jax.ShapeDtypeStruct((LAYERS, 896), jnp.float32)),
        in_specs=[WHOLE, WHOLE, WHOLE] + [WHOLE] * 7,
        out_specs=(WHOLE, WHOLE),
        scratch_shapes=[
            room(2, 280, 128),
            room(LAYERS, 2, 2, FAR_WINDOW + 16, 128),
            room(2, 2, 408, 128),
            room(LAYERS - 1, 2, 2, 144 + 16, 128),
            room(LAYERS, 160, 128),
            *SCALARS,
        ],
        input_output_aliases={9: 0},
        name="left_far",
        **limits(10_000_000, 8 * 2**20),
    )(pairing, offsets, weights, before, before_far, states, table, halo_table, rest, adjoint)


def right_call(*operands):
    return pl.pallas_call(
        right_kernel,
        out_shape=(EVOLVED, STATES, ADJOINT, TABLE, HALO_TABLE, jax.ShapeDtypeStruct((LAYERS, 768), jnp.float32)),
        in_specs=[WHOLE, WHOLE, WHOLE, FAR] + [WHOLE] * 3 + [FAR, WHOLE, WHOLE, WHOLE],
        out_specs=(FAR, WHOLE, WHOLE, WHOLE, WHOLE, WHOLE),
        scratch_shapes=[
            room(2, 2 * RIGHT_WINDOW + 8, 128),
            room(LAYERS, 2, 2, RIGHT_WINDOW + 16, 128),
            room(2, 2, 560, 128),
            room(LAYERS - 1, 2, 2, 144 + 16, 128),
            room(LAYERS, 168, 128),
            room(2, 40, 128),
            pltpu.SemaphoreType.DMA((6,)),
            *SCALARS,
        ],
        input_output_aliases={7: 0, 8: 1, 9: 2, 10: 3},
        name="right",
        **limits(15_000_000, 8 * 2**20),
    )(*operands)


def right_far_call(*operands):
    return pl.pallas_call(
        right_far_kernel,
        out_shape=(ADJOINT, jax.ShapeDtypeStruct((LAYERS, PAIRS), jnp.float32)),
        in_specs=[WHOLE, WHOLE, WHOLE] + [WHOLE] * 7,
        out_specs=(WHOLE, WHOLE),
        scratch_shapes=[
            room(2, 2 * RIGHT_FAR_WINDOW + 8, 128),
            room(LAYERS, 2, 2, RIGHT_FAR_WINDOW + 16, 128),
            room(2, 2, 440, 128),
            room(LAYERS - 1, 2, 2, 160 + 16, 128),
            room(LAYERS, 176, 128),
            *SCALARS,
        ],
        input_output_aliases={9: 0},
        name="right_far",
        **limits(10_000_000, 8 * 2**20),
    )(*operands)


def on_device(slab, angles, pairing, band_offsets, band_weights):
    count = lax.axis_size("blk")
    onward = [(i, (i + 1) % count) for i in range(count)]
    back = [((i + 1) % count, i) for i in range(count)]
    scalars = [pltpu.with_memory_space_constraint(x, pltpu.HBM) for x in (pairing, band_offsets, band_weights)]
    tail, far_tail, head, far_head, *scalars, angles_near = pack_call(
        slab, angles, ((ROWS - NEAR, NEAR, 512), (ROWS - NEAR - SENT, SENT, None), (0, HEAD, 0), (HEAD, HALO - HEAD, None)),
        *scalars,
    )
    before = lax.ppermute(tail, "blk", onward)
    before_far = lax.ppermute(far_tail, "blk", onward)
    states, table, head, far_head = early_call(scalars[0], slab, angles_near, head, far_head)
    after = lax.ppermute(head, "blk", back)
    after_far = lax.ppermute(far_head, "blk", back)
    states, table = later_call(scalars[0], slab, angles_near, states, table)
    evolved, states, adjoint, inner = inner_call(*scalars, states, table)
    evolved, states, adjoint, table, left_table, left = left_call(
        *scalars, slab, before, evolved, states, adjoint, table, inner
    )
    evolved, states, adjoint, table, right_table, rest = right_call(
        *scalars, slab, after, inner, left, evolved, states, adjoint, table
    )
    adjoint, rest = left_far_call(*scalars, before, before_far, states, table, left_table, rest, adjoint)
    _, gradient = right_far_call(*scalars, after, after_far, states, table, right_table, rest, adjoint)
    columns = lax.axis_size("col")
    step = 1
    while step < columns:
        gradient = gradient + lax.ppermute(gradient, "col", [(i, i ^ step) for i in range(columns)])
        step *= 2
    return (evolved, gradient)


def solution(mesh):
    in_specs = (P("blk", "col"), P(None, "blk"), P(), P(), P())
    out_specs = (P("blk", "col"), P(None, "blk"))
    return jax.shard_map(
        on_device, mesh=mesh, in_specs=in_specs, out_specs=out_specs, check_vma=False
    )
```

```python
import jax
import jax.numpy as jnp
from jax import lax
from jax.experimental import pallas as pl
from jax.experimental.pallas import tpu as pltpu
from jax.sharding import PartitionSpec as P

LAYERS = 4
REACH = 512
BANDS = 8
ROWS = 2048
PAIRS = 1024
NEAR = 280
FAR_ROWS = 240
HALO = NEAR + FAR_ROWS
SENT = 272
HEAD = 256
EARLY = 2
PAD = 272
LENGTH = PAD + PAIRS + PAD
WINDOW = 160
FAR_WINDOW = 136
RIGHT_WINDOW = 144
RIGHT_FAR_WINDOW = 152
FRONT = 8
GFRONT = 8


def fill_table(table, at, angle, low=0, high=128):
    both = jnp.concatenate([jnp.cos(angle), jnp.sin(angle)], 0)
    tall = jnp.transpose(both)
    for lane in range(2 * LAYERS):
        table[lane, pl.ds(at, high - low), :] = jnp.broadcast_to(tall[low:high, lane : lane + 1], (high - low, 128))


def forward(raw, states, start, table, table_start, lead, pairs, step):
    for layer in range(LAYERS):
        odd = layer % 2

        def block(i, carry, layer=layer, odd=odd):
            at = pl.multiple_of(i * step, 8)
            angle_at = at + table_start + lead if odd else at + table_start
            cosine = table[layer, pl.ds(angle_at, step), :]
            sine = table[LAYERS + layer, pl.ds(angle_at, step), :]
            for half in range(2):
                if layer == 0:
                    first = raw[half, pl.ds(2 * at + lead, step, stride=2), :]
                    second = raw[half, pl.ds(2 * at + lead + 1, step, stride=2), :]
                elif odd:
                    first = states[layer - 1, 1, half, pl.ds(at + start, step), :]
                    second = states[layer - 1, 0, half, pl.ds(at + start + 1, step), :]
                else:
                    first = states[layer - 1, 0, half, pl.ds(at + start - 1, step), :]
                    second = states[layer - 1, 1, half, pl.ds(at + start, step), :]
                states[layer, odd, half, pl.ds(at + start, step), :] = cosine * first - sine * second
                states[layer, 1 - odd, half, pl.ds(at + start, step), :] = sine * first + cosine * second
            return carry

        lax.fori_loop(0, pairs // step, block, 0)


def band(source, source_start, total, total_start, offsets, weights, pairs, step, signs, add):
    where = []
    for parity in range(2):
        for k in range(BANDS):
            for sign in signs:
                row = parity + sign * offsets[k]
                side = lax.bitwise_and(row, 1)
                where.append((side, lax.shift_right_arithmetic(row, 1) - 1 + side + source_start))

    def block(i, carry):
        at = pl.multiple_of(i * step, 8)
        for parity in range(2):
            for half in range(2):
                place = (parity, half, pl.ds(at + total_start, step), slice(None))
                value = total[place] if add else None
                for k in range(BANDS):
                    term = None
                    for n in range(len(signs)):
                        side, shift = where[(parity * BANDS + k) * len(signs) + n]
                        row = source[side, half, pl.ds(at + shift, step), :]
                        term = row if term is None else term + row
                    term = weights[k] * term
                    value = term if value is None else value + term
                total[place] = value
        return carry

    lax.fori_loop(0, pairs // step, block, 0)


def backward(states, start, adjoint, adjoint_start, turned, products, table, table_start, lead, pairs, step):
    for layer in reversed(range(LAYERS)):
        odd = layer % 2

        def block(i, carry, layer=layer, odd=odd):
            at = pl.multiple_of(i * step, 8)
            angle_at = at + table_start + lead if odd else at + table_start
            cosine = table[layer, pl.ds(angle_at, step), :]
            sine = table[LAYERS + layer, pl.ds(angle_at, step), :]
            product = None
            for half in range(2):
                source = adjoint if layer == LAYERS - 1 else turned.at[layer]
                begin = adjoint_start if layer == LAYERS - 1 else FRONT
                if odd:
                    first = source[1, half, pl.ds(at + begin, step), :]
                    second = source[0, half, pl.ds(at + begin + 1, step), :]
                else:
                    first = source[0, half, pl.ds(at + begin - 1, step), :]
                    second = source[1, half, pl.ds(at + begin, step), :]
                state_first = states[layer, odd, half, pl.ds(at + start, step), :]
                state_second = states[layer, 1 - odd, half, pl.ds(at + start, step), :]
                part = second * state_first - first * state_second
                product = part if product is None else product + part
                if layer:
                    turned[layer - 1, odd, half, pl.ds(at + FRONT, step), :] = cosine * first + sine * second
                    turned[layer - 1, 1 - odd, half, pl.ds(at + FRONT, step), :] = cosine * second - sine * first
            products[layer, pl.ds(at + GFRONT, step), :] = product
            return carry

        lax.fori_loop(0, pairs // step, block, 0)


def summed(products, lead, at):
    rows = []
    for layer in range(LAYERS):
        block = products[layer, pl.ds(at + GFRONT - lead if layer % 2 else at + GFRONT, 128), :]
        rows.append(jnp.sum(jnp.transpose(block), axis=0, keepdims=True))
    return jnp.concatenate(rows, 0)


def fetching(sources, scalars):
    copies = [pltpu.make_async_copy(source, scalars[n], scalars[3].at[n]) for n, source in enumerate(sources)]
    for copy in copies:
        copy.start()
    return copies


def fetched(sources, scalars):
    for copy in fetching(sources, scalars):
        copy.wait()
    return scalars[:3]


def evolve(pairing, slab, angles, states, table, raw, flags, sems):
    scalar = pltpu.make_async_copy(pairing, flags, sems.at[2])
    scalar.start()
    loads = []
    for half in range(2):
        loads.append(pltpu.make_async_copy(slab.at[:, pl.ds(128 * half, 128)], raw.at[half, pl.ds(0, ROWS), :], sems.at[half]))
        loads[-1].start()
    for tile in range(8):
        fill_table(table, FRONT + 128 * tile, angles[:, 128 * tile : 128 * (tile + 1)])
    for load in loads:
        load.wait()
    scalar.wait()
    forward(raw, states, PAD, table, FRONT, flags[0], PAIRS, 128)


def early_kernel(pairing, slab, angles, head_in, far_head_in, states, table, head, far_head, raw, flags, sems):
    @pl.when(lax.axis_index("blk") < EARLY)
    def _():
        evolve(pairing, slab, angles, states, table, raw, flags, sems)


def later_kernel(pairing, slab, angles, states_in, table_in, states, table, raw, flags, sems):
    @pl.when(lax.axis_index("blk") >= EARLY)
    def _():
        evolve(pairing, slab, angles, states, table, raw, flags, sems)


def inner_kernel(
    pairing, offsets, weights, states_in, table, evolved, states, adjoint, gradient, turned, products, out, sems, *scalars
):
    pairing, offsets, weights = fetched((pairing, offsets, weights), scalars)
    lead = pairing[0]

    def weave(i, carry):
        at = pl.multiple_of(i * 128, 128)
        for half in range(2):
            out[half, pl.ds(2 * at + lead + FRONT, 128, stride=2), :] = states[3, 0, half, pl.ds(at + PAD - 1, 128), :]
            out[half, pl.ds(2 * at + lead + FRONT + 1, 128, stride=2), :] = states[3, 1, half, pl.ds(at + PAD, 128), :]
        return carry

    lax.fori_loop(0, PAIRS // 128, weave, 0)
    stores = []
    for half in range(2):
        stores.append(
            pltpu.make_async_copy(out.at[half, pl.ds(FRONT, ROWS), :], evolved.at[:, pl.ds(128 * half, 128)], sems.at[half])
        )
        stores[-1].start()
    blank = jnp.zeros((PAD + 8, 128), jnp.float32)
    for parity in range(2):
        for half in range(2):
            states[LAYERS - 1, parity, half, pl.ds(0, PAD + 8), :] = blank
            states[LAYERS - 1, parity, half, pl.ds(PAD + PAIRS - 8, PAD + 8), :] = blank
    last = states.at[LAYERS - 1]
    band(last, PAD - 8, adjoint, FRONT, offsets, weights, PAIRS + 16, 104, (1, -1), False)
    backward(states, PAD + 256, adjoint, FRONT + 8 + 256, turned, products, table, FRONT + 256, lead, 512, 128)
    for tile in range(4):
        gradient[:, 128 * tile : 128 * (tile + 1)] = summed(products, lead, 128 * tile)
    for store in stores:
        store.wait()


def halo_angles(halo, at, tile):
    return halo[at + 4 * (tile // 2) : at + 4 * (tile // 2) + 4, 128 * (tile % 2) : 128 * (tile % 2) + 128]


def placed(pieces, raw):
    for piece, piece_at, at, rows in pieces:
        for half in range(2):
            raw[half, pl.ds(at, rows), :] = piece[pl.ds(piece_at, rows), 128 * half : 128 * half + 128]


def started(pieces, raw, sems):
    loads = []
    for half in range(2):
        for piece, piece_at, at, rows in pieces:
            load = pltpu.make_async_copy(
                piece.at[pl.ds(piece_at, rows), pl.ds(128 * half, 128)], raw.at[half, pl.ds(at, rows), :], sems.at[len(loads)]
            )
            load.start()
            loads.append(load)
    return loads


def near_tables(side, halo, at, table, halo_table):
    if side == 0:
        fill_table(halo_table, 0, halo_angles(halo, at, 1), 120, 128)
        fill_table(halo_table, 8, halo_angles(halo, at, 2))
        fill_table(halo_table, 136, halo_angles(halo, at, 3))
    else:
        fill_table(halo_table, 16, halo_angles(halo, at, 0))
        fill_table(halo_table, 144, halo_angles(halo, at, 1))
        fill_table(halo_table, 272, halo_angles(halo, at, 2), 0, 16)
    for lane in range(2 * LAYERS):
        if side == 0:
            halo_table[lane, pl.ds(264, 24), :] = table[lane, pl.ds(FRONT, 24), :]
            table[lane, pl.ds(0, FRONT), :] = halo_table[lane, pl.ds(256, 8), :]
        else:
            halo_table[lane, pl.ds(0, 16), :] = table[lane, pl.ds(FRONT + PAIRS - 16, 16), :]
            table[lane, pl.ds(FRONT + PAIRS, 16), :] = halo_table[lane, pl.ds(16, 16), :]


def boundary(side, at, lead, window, states, out, evolved, sems):
    stores = []
    for half in range(2):
        out[half, pl.ds(lead, 16, stride=2), :] = window[3, 0, half, pl.ds(at - 9, 16), :]
        out[half, pl.ds(lead + 1, 16, stride=2), :] = window[3, 1, half, pl.ds(at - 8, 16), :]
        store = pltpu.make_async_copy(
            out.at[half, pl.ds(16, 16), :],
            evolved.at[pl.ds((0, ROWS - 16)[side], 16), pl.ds(128 * half, 128)],
            sems.at[half],
        )
        store.start()
        stores.append(store)
        for parity in range(2):
            for layer in range(LAYERS):
                states[layer, parity, half, pl.ds(PAD + (-8, PAIRS - 8)[side], 16), :] = window[
                    layer, parity, half, pl.ds(at + (-8, 0)[side], 16), :
                ]
    return stores


def left_kernel(
    pairing, offsets, weights, slab, before, evolved_in, states_in, adjoint_in, table_in, inner,
    evolved, states, adjoint, table, halo_table, gradient, raw, window, source, turned, products, out, sems, *scalars,
):
    copies = fetching((pairing, offsets, weights), scalars)
    loads = started(((slab, 0, 8 + NEAR, 40),), raw, sems)
    placed(((before, 0, 8, NEAR),), raw)
    near_tables(0, before, NEAR, table, halo_table)
    for load in loads + copies:
        load.wait()
    pairing, offsets, weights = scalars[:3]
    lead = pairing[0]
    forward(raw, window, FRONT, halo_table, 120, lead, WINDOW, 80)
    stores = boundary(0, FRONT + 144, lead, window, states, out, evolved, sems.at[pl.ds(4, 2)])
    blank = jnp.zeros((272, 128), jnp.float32)
    for half in range(2):
        for parity in range(2):
            source[parity, half, pl.ds(0, 136), :] = blank[:136]
            source[parity, half, pl.ds(136, 144), :] = window[3, parity, half, pl.ds(FRONT + 8, 144), :]
            source[parity, half, pl.ds(280, 272), :] = blank
    band(source, 264, adjoint, FRONT, offsets, weights, 288, 96, (-1,), True)
    band(source, 264, adjoint, FRONT, offsets, weights, 16, 16, (1,), True)
    backward(states, PAD + 120, adjoint, FRONT + 8 + 120, turned, products, table, FRONT + 120, lead, 160, 80)
    lane = lax.broadcasted_iota(jnp.int32, (LAYERS, 128), 1)
    gradient[:, 0:128] = summed(products, lead, 8)
    gradient[:, 128:256] = jnp.where(lane < 16, summed(products, lead, 136), inner[:, 0:128])
    gradient[:, 256:512] = inner[:, 128:384]
    for store in stores:
        store.wait()


def left_far_kernel(
    pairing, offsets, weights, before, before_far, states, table, halo_table, rest, adjoint_in,
    adjoint, gradient, raw, window, source, turned, products, *scalars,
):
    copies = fetching((pairing, offsets, weights), scalars)
    placed(((before_far, SENT - FAR_ROWS, 8, FAR_ROWS), (before, 0, 8 + FAR_ROWS, 32)), raw)
    blank = jnp.zeros((272, 128), jnp.float32)
    for half in range(2):
        for parity in range(2):
            source[parity, half, pl.ds(136, 272), :] = blank
    gradient[:, 128:896] = rest[...]
    for load in copies:
        load.wait()
    pairing, offsets, weights = scalars[:3]
    lead = pairing[0]
    forward(raw, window, FRONT, halo_table, 0, lead, FAR_WINDOW, 136)
    for half in range(2):
        for parity in range(2):
            source[parity, half, pl.ds(8, 128), :] = window[3, parity, half, pl.ds(FRONT, 128), :]
    band(source, 264, adjoint, FRONT, offsets, weights, 144, 144, (-1,), True)
    backward(states, PAD - 8, adjoint, FRONT, turned, products, table, FRONT - 8, lead, 144, 144)
    gradient[:, 0:128] = summed(products, lead, 8)


def right_kernel(
    pairing, offsets, weights, slab, after, inner, left, evolved_in, states_in, adjoint_in, table_in,
    evolved, states, adjoint, table, halo_table, gradient, raw, window, source, turned, products, out, sems, *scalars,
):
    copies = fetching((pairing, offsets, weights), scalars)
    loads = started(((slab, ROWS - 32, 0, 32),), raw, sems)
    placed(((after, 0, 32, HEAD),), raw)
    near_tables(1, after, HEAD, table, halo_table)
    blank = jnp.zeros((272, 128), jnp.float32)
    for half in range(2):
        for parity in range(2):
            source[parity, half, pl.ds(0, 272), :] = blank
            source[parity, half, pl.ds(400, 152), :] = blank[:152]
    gradient[:, 0:512] = left[...]
    for load in loads + copies:
        load.wait()
    pairing, offsets, weights = scalars[:3]
    lead = pairing[0]
    forward(raw, window, FRONT, halo_table, 0, lead, RIGHT_WINDOW, 72)
    stores = boundary(1, FRONT + 8, lead, window, states, out, evolved, sems.at[pl.ds(4, 2)])
    for half in range(2):
        for parity in range(2):
            source[parity, half, pl.ds(272, 128), :] = window[3, parity, half, pl.ds(FRONT + 8, 128), :]
    band(source, 0, adjoint, FRONT + 752, offsets, weights, 288, 144, (1,), True)
    band(source, 272, adjoint, FRONT + PAIRS, offsets, weights, 16, 16, (-1,), True)
    backward(states, PAD + 744, adjoint, FRONT + 8 + 744, turned, products, table, FRONT + 744, lead, 144, 144)
    lane = lax.broadcasted_iota(jnp.int32, (LAYERS, 128), 1)
    gradient[:, 512:640] = jnp.where(lane < 112, inner[:, 384:512], pltpu.roll(summed(products, lead, 8), 112, 1))
    gradient[:, 640:768] = summed(products, lead, 24)
    for store in stores:
        store.wait()


def right_far_kernel(
    pairing, offsets, weights, after, after_far, states, table, halo_table, rest, adjoint_in,
    adjoint, gradient, raw, window, source, turned, products, *scalars,
):
    copies = fetching((pairing, offsets, weights), scalars)
    placed(((after, HEAD - 32, 0, 32), (after_far, 0, 32, HALO - HEAD)), raw)
    blank = jnp.zeros((272, 128), jnp.float32)
    for half in range(2):
        for parity in range(2):
            source[parity, half, pl.ds(0, 272), :] = blank
    gradient[:, 0:768] = rest[:, 0:768]
    for load in copies:
        load.wait()
    pairing, offsets, weights = scalars[:3]
    lead = pairing[0]
    forward(raw, window, FRONT, halo_table, 128, lead, RIGHT_FAR_WINDOW, 152)
    for half in range(2):
        for parity in range(2):
            source[parity, half, pl.ds(272, 144), :] = window[3, parity, half, pl.ds(FRONT + 8, 144), :]
    band(source, 0, adjoint, FRONT + 880, offsets, weights, 160, 160, (1,), True)
    backward(states, PAD + 872, adjoint, FRONT + 8 + 872, turned, products, table, FRONT + 872, lead, 160, 160)
    lane = lax.broadcasted_iota(jnp.int32, (LAYERS, 128), 1)
    gradient[:, 768:896] = jnp.where(lane < 112, rest[:, 768:896], pltpu.roll(summed(products, lead, 8), 112, 1))
    gradient[:, 896:1024] = summed(products, lead, 24)


WHOLE = pl.BlockSpec(memory_space=pltpu.VMEM)
FAR = pl.BlockSpec(memory_space=pl.ANY)

EVOLVED = jax.ShapeDtypeStruct((ROWS, 256), jnp.float32)
STATES = jax.ShapeDtypeStruct((LAYERS, 2, 2, LENGTH, 128), jnp.float32)
ADJOINT = jax.ShapeDtypeStruct((2, 2, PAIRS + 32, 128), jnp.float32)
TABLE = jax.ShapeDtypeStruct((2 * LAYERS, PAIRS + 32, 128), jnp.float32)
HALO_TABLE = jax.ShapeDtypeStruct((2 * LAYERS, 304, 128), jnp.float32)


def limits(flops, traffic, grant=16):
    return dict(
        compiler_params=pltpu.CompilerParams(vmem_limit_bytes=grant * 2**20),
        cost_estimate=pl.CostEstimate(flops=flops, bytes_accessed=traffic, transcendentals=8192),
    )


def room(*shape):
    return pltpu.VMEM(shape, jnp.float32)


def pack_call(slab, angles, pieces, *scalars):
    shapes = [(rows + (0 if lane is None else 8), 256) for _, rows, lane in pieces]

    def kernel(slab, angles, *refs):
        count = len(scalars)
        sources, packed, kept = refs[:count], refs[count : count + len(pieces)], refs[count + len(pieces) : -2]
        tiles, sems = refs[-2], refs[-1]
        copies = [pltpu.make_async_copy(angles, tiles, sems.at[len(pieces)])]
        for n, source in enumerate(sources):
            copies.append(pltpu.make_async_copy(source, kept[n], sems.at[len(pieces) + 1 + n]))
        for n, (first, rows, _) in enumerate(pieces):
            copies.append(
                pltpu.make_async_copy(slab.at[pl.ds(first, rows), :], packed[n].at[pl.ds(0, rows), :], sems.at[n])
            )
        for copy in copies:
            copy.start()
        copies[0].wait()
        for n, (_, rows, lane) in enumerate(pieces):
            if lane is not None:
                for row in range(2):
                    lanes = slice(lane + 256 * row, lane + 256 * (row + 1))
                    packed[n][rows + 4 * row : rows + 4 * (row + 1), :] = tiles[:, lanes]
        for copy in copies[1:]:
            copy.wait()

    return pl.pallas_call(
        kernel,
        out_shape=[jax.ShapeDtypeStruct(shape, jnp.float32) for shape in shapes]
        + [jax.ShapeDtypeStruct(x.shape, x.dtype) for x in (*scalars, angles)],
        in_specs=[pl.BlockSpec(memory_space=pltpu.HBM)] * (2 + len(scalars)),
        out_specs=[WHOLE] * (len(pieces) + len(scalars) + 1),
        scratch_shapes=[pltpu.SemaphoreType.DMA((len(pieces) + len(scalars) + 1,))],
        name="pack",
        **limits(1000, 2**20),
    )(slab, angles, *scalars)


SCALARS = [
    pltpu.SMEM((LAYERS,), jnp.int32),
    pltpu.SMEM((BANDS,), jnp.int32),
    pltpu.SMEM((BANDS,), jnp.float32),
    pltpu.SemaphoreType.DMA((3,)),
]
EVOLVE_ROOM = [room(2, ROWS + 8, 128), pltpu.SMEM((LAYERS,), jnp.int32), pltpu.SemaphoreType.DMA((3,))]


def early_call(pairing, slab, angles, head, far_head):
    return pl.pallas_call(
        early_kernel,
        out_shape=(STATES, TABLE) + tuple(jax.ShapeDtypeStruct(x.shape, x.dtype) for x in (head, far_head)),
        in_specs=[WHOLE, FAR, WHOLE, FAR, FAR],
        out_specs=(WHOLE, WHOLE, FAR, FAR),
        scratch_shapes=EVOLVE_ROOM,
        input_output_aliases={3: 2, 4: 3},
        name="early",
        **limits(12_000_000, 8 * 2**20),
    )(pairing, slab, angles, head, far_head)


def later_call(pairing, slab, angles, states, table):
    return pl.pallas_call(
        later_kernel,
        out_shape=(STATES, TABLE),
        in_specs=[WHOLE, FAR, WHOLE, WHOLE, WHOLE],
        out_specs=(WHOLE, WHOLE),
        scratch_shapes=EVOLVE_ROOM,
        input_output_aliases={3: 0, 4: 1},
        name="later",
        **limits(12_000_000, 8 * 2**20),
    )(pairing, slab, angles, states, table)


def inner_call(pairing, offsets, weights, states, table):
    return pl.pallas_call(
        inner_kernel,
        out_shape=(EVOLVED, STATES, ADJOINT, jax.ShapeDtypeStruct((LAYERS, 512), jnp.float32)),
        in_specs=[WHOLE, WHOLE, WHOLE, WHOLE, WHOLE],
        out_specs=(FAR, WHOLE, WHOLE, WHOLE),
        scratch_shapes=[
            room(LAYERS - 1, 2, 2, 512 + 16, 128),
            room(LAYERS, 512 + 16, 128),
            room(2, ROWS + 16, 128),
            pltpu.SemaphoreType.DMA((2,)),
            *SCALARS,
        ],
        input_output_aliases={3: 1},
        name="inner",
        **limits(50_000_000, 16 * 2**20),
    )(pairing, offsets, weights, states, table)


def left_call(pairing, offsets, weights, slab, before, evolved, states, adjoint, table, inner):
    return pl.pallas_call(
        left_kernel,
        out_shape=(EVOLVED, STATES, ADJOINT, TABLE, HALO_TABLE, jax.ShapeDtypeStruct((LAYERS, 512), jnp.float32)),
        in_specs=[WHOLE, WHOLE, WHOLE, FAR, WHOLE, FAR, WHOLE, WHOLE, WHOLE, WHOLE],
        out_specs=(FAR, WHOLE, WHOLE, WHOLE, WHOLE, WHOLE),
        scratch_shapes=[
            room(2, 328, 128),
            room(LAYERS, 2, 2, WINDOW + 16, 128),
            room(2, 2, 552, 128),
            room(LAYERS - 1, 2, 2, 160 + 16, 128),
            room(LAYERS, 280, 128),
            room(2, 40, 128),
            pltpu.SemaphoreType.DMA((6,)),
            *SCALARS,
        ],
        input_output_aliases={5: 0, 6: 1, 7: 2, 8: 3},
        name="left",
        **limits(15_000_000, 8 * 2**20),
    )(pairing, offsets, weights, slab, before, evolved, states, adjoint, table, inner)


def left_far_call(pairing, offsets, weights, before, before_far, states, table, halo_table, rest, adjoint):
    return pl.pallas_call(
        left_far_kernel,
        out_shape=(ADJOINT, jax.ShapeDtypeStruct((LAYERS, 896), jnp.float32)),
        in_specs=[WHOLE, WHOLE, WHOLE] + [WHOLE] * 7,
        out_specs=(WHOLE, WHOLE),
        scratch_shapes=[
            room(2, 280, 128),
            room(LAYERS, 2, 2, FAR_WINDOW + 16, 128),
            room(2, 2, 408, 128),
            room(LAYERS - 1, 2, 2, 144 + 16, 128),
            room(LAYERS, 160, 128),
            *SCALARS,
        ],
        input_output_aliases={9: 0},
        name="left_far",
        **limits(10_000_000, 8 * 2**20),
    )(pairing, offsets, weights, before, before_far, states, table, halo_table, rest, adjoint)


def right_call(*operands):
    return pl.pallas_call(
        right_kernel,
        out_shape=(EVOLVED, STATES, ADJOINT, TABLE, HALO_TABLE, jax.ShapeDtypeStruct((LAYERS, 768), jnp.float32)),
        in_specs=[WHOLE, WHOLE, WHOLE, FAR] + [WHOLE] * 3 + [FAR, WHOLE, WHOLE, WHOLE],
        out_specs=(FAR, WHOLE, WHOLE, WHOLE, WHOLE, WHOLE),
        scratch_shapes=[
            room(2, 2 * RIGHT_WINDOW + 8, 128),
            room(LAYERS, 2, 2, RIGHT_WINDOW + 16, 128),
            room(2, 2, 560, 128),
            room(LAYERS - 1, 2, 2, 144 + 16, 128),
            room(LAYERS, 168, 128),
            room(2, 40, 128),
            pltpu.SemaphoreType.DMA((6,)),
            *SCALARS,
        ],
        input_output_aliases={7: 0, 8: 1, 9: 2, 10: 3},
        name="right",
        **limits(15_000_000, 8 * 2**20),
    )(*operands)


def right_far_call(*operands):
    return pl.pallas_call(
        right_far_kernel,
        out_shape=(ADJOINT, jax.ShapeDtypeStruct((LAYERS, PAIRS), jnp.float32)),
        in_specs=[WHOLE, WHOLE, WHOLE] + [WHOLE] * 7,
        out_specs=(WHOLE, WHOLE),
        scratch_shapes=[
            room(2, 2 * RIGHT_FAR_WINDOW + 8, 128),
            room(LAYERS, 2, 2, RIGHT_FAR_WINDOW + 16, 128),
            room(2, 2, 440, 128),
            room(LAYERS - 1, 2, 2, 160 + 16, 128),
            room(LAYERS, 176, 128),
            *SCALARS,
        ],
        input_output_aliases={9: 0},
        name="right_far",
        **limits(10_000_000, 8 * 2**20),
    )(*operands)


def on_device(slab, angles, pairing, band_offsets, band_weights):
    slab = pltpu.with_memory_space_constraint(slab, pltpu.HBM)
    angles = pltpu.with_memory_space_constraint(angles, pltpu.HBM)
    count = lax.axis_size("blk")
    onward = [(i, (i + 1) % count) for i in range(count)]
    back = [((i + 1) % count, i) for i in range(count)]
    scalars = [pltpu.with_memory_space_constraint(x, pltpu.HBM) for x in (pairing, band_offsets, band_weights)]
    tail, far_tail, head, far_head, *scalars, angles_near = pack_call(
        slab, angles, ((ROWS - NEAR, NEAR, 512), (ROWS - NEAR - SENT, SENT, None), (0, HEAD, 0), (HEAD, HALO - HEAD, None)),
        *scalars,
    )
    before = lax.ppermute(tail, "blk", onward)
    before_far = lax.ppermute(far_tail, "blk", onward)
    states, table, head, far_head = early_call(scalars[0], slab, angles_near, head, far_head)
    after = lax.ppermute(head, "blk", back)
    after_far = lax.ppermute(far_head, "blk", back)
    states, table = later_call(scalars[0], slab, angles_near, states, table)
    evolved, states, adjoint, inner = inner_call(*scalars, states, table)
    evolved, states, adjoint, table, left_table, left = left_call(
        *scalars, slab, before, evolved, states, adjoint, table, inner
    )
    evolved, states, adjoint, table, right_table, rest = right_call(
        *scalars, slab, after, inner, left, evolved, states, adjoint, table
    )
    adjoint, rest = left_far_call(*scalars, before, before_far, states, table, left_table, rest, adjoint)
    _, gradient = right_far_call(*scalars, after, after_far, states, table, right_table, rest, adjoint)
    columns = lax.axis_size("col")
    step = 1
    while step < columns:
        gradient = gradient + lax.ppermute(gradient, "col", [(i, i ^ step) for i in range(columns)])
        step *= 2
    return (evolved, gradient)


def solution(mesh):
    in_specs = (P("blk", "col"), P(None, "blk"), P(), P(), P())
    out_specs = (P("blk", "col"), P(None, "blk"))
    return jax.shard_map(
        on_device, mesh=mesh, in_specs=in_specs, out_specs=out_specs, check_vma=False
    )
```

```python
import jax
import jax.numpy as jnp
from jax import lax
from jax.experimental import pallas as pl
from jax.experimental.pallas import tpu as pltpu
from jax.sharding import PartitionSpec as P

LAYERS = 4
REACH = 512
BANDS = 8
ROWS = 2048
PAIRS = 1024
NEAR = 280
FAR_ROWS = 240
HALO = NEAR + FAR_ROWS
SENT = 272
HEAD = 256
EARLY = 2
PAD = 272
LENGTH = PAD + PAIRS + PAD
WINDOW = 160
FAR_WINDOW = 136
RIGHT_WINDOW = 144
RIGHT_FAR_WINDOW = 152
FRONT = 8
GFRONT = 8


def fill_table(table, at, angle, low=0, high=128):
    both = jnp.concatenate([jnp.cos(angle), jnp.sin(angle)], 0)
    tall = jnp.transpose(both)
    for lane in range(2 * LAYERS):
        table[lane, pl.ds(at, high - low), :] = jnp.broadcast_to(tall[low:high, lane : lane + 1], (high - low, 128))


def forward(raw, states, start, table, table_start, lead, pairs, step):
    for layer in range(LAYERS):
        odd = layer % 2

        def block(i, carry, layer=layer, odd=odd):
            at = pl.multiple_of(i * step, 8)
            angle_at = at + table_start + lead if odd else at + table_start
            cosine = table[layer, pl.ds(angle_at, step), :]
            sine = table[LAYERS + layer, pl.ds(angle_at, step), :]
            for half in range(2):
                if layer == 0:
                    first = raw[half, pl.ds(2 * at + lead, step, stride=2), :]
                    second = raw[half, pl.ds(2 * at + lead + 1, step, stride=2), :]
                elif odd:
                    first = states[layer - 1, 1, half, pl.ds(at + start, step), :]
                    second = states[layer - 1, 0, half, pl.ds(at + start + 1, step), :]
                else:
                    first = states[layer - 1, 0, half, pl.ds(at + start - 1, step), :]
                    second = states[layer - 1, 1, half, pl.ds(at + start, step), :]
                states[layer, odd, half, pl.ds(at + start, step), :] = cosine * first - sine * second
                states[layer, 1 - odd, half, pl.ds(at + start, step), :] = sine * first + cosine * second
            return carry

        lax.fori_loop(0, pairs // step, block, 0)


def band(source, source_start, total, total_start, offsets, weights, pairs, step, signs, add):
    where = []
    for parity in range(2):
        for k in range(BANDS):
            for sign in signs:
                row = parity + sign * offsets[k]
                side = lax.bitwise_and(row, 1)
                where.append((side, lax.shift_right_arithmetic(row, 1) - 1 + side + source_start))

    def block(i, carry):
        at = pl.multiple_of(i * step, 8)
        for parity in range(2):
            for half in range(2):
                place = (parity, half, pl.ds(at + total_start, step), slice(None))
                value = total[place] if add else None
                for k in range(BANDS):
                    term = None
                    for n in range(len(signs)):
                        side, shift = where[(parity * BANDS + k) * len(signs) + n]
                        row = source[side, half, pl.ds(at + shift, step), :]
                        term = row if term is None else term + row
                    term = weights[k] * term
                    value = term if value is None else value + term
                total[place] = value
        return carry

    lax.fori_loop(0, pairs // step, block, 0)


def backward(states, start, adjoint, adjoint_start, turned, products, table, table_start, lead, pairs, step):
    for layer in reversed(range(LAYERS)):
        odd = layer % 2

        def block(i, carry, layer=layer, odd=odd):
            at = pl.multiple_of(i * step, 8)
            angle_at = at + table_start + lead if odd else at + table_start
            cosine = table[layer, pl.ds(angle_at, step), :]
            sine = table[LAYERS + layer, pl.ds(angle_at, step), :]
            product = None
            for half in range(2):
                source = adjoint if layer == LAYERS - 1 else turned.at[layer]
                begin = adjoint_start if layer == LAYERS - 1 else FRONT
                if odd:
                    first = source[1, half, pl.ds(at + begin, step), :]
                    second = source[0, half, pl.ds(at + begin + 1, step), :]
                else:
                    first = source[0, half, pl.ds(at + begin - 1, step), :]
                    second = source[1, half, pl.ds(at + begin, step), :]
                state_first = states[layer, odd, half, pl.ds(at + start, step), :]
                state_second = states[layer, 1 - odd, half, pl.ds(at + start, step), :]
                part = second * state_first - first * state_second
                product = part if product is None else product + part
                if layer:
                    turned[layer - 1, odd, half, pl.ds(at + FRONT, step), :] = cosine * first + sine * second
                    turned[layer - 1, 1 - odd, half, pl.ds(at + FRONT, step), :] = cosine * second - sine * first
            products[layer, pl.ds(at + GFRONT, step), :] = product
            return carry

        lax.fori_loop(0, pairs // step, block, 0)


def summed(products, lead, at):
    rows = []
    for layer in range(LAYERS):
        block = products[layer, pl.ds(at + GFRONT - lead if layer % 2 else at + GFRONT, 128), :]
        rows.append(jnp.sum(jnp.transpose(block), axis=0, keepdims=True))
    return jnp.concatenate(rows, 0)


def fetching(sources, scalars):
    copies = [pltpu.make_async_copy(source, scalars[n], scalars[3].at[n]) for n, source in enumerate(sources)]
    for copy in copies:
        copy.start()
    return copies


def fetched(sources, scalars):
    for copy in fetching(sources, scalars):
        copy.wait()
    return scalars[:3]


def evolve(pairing, slab, angles, states, table, raw, flags, sems):
    scalar = pltpu.make_async_copy(pairing, flags, sems.at[2])
    scalar.start()
    loads = []
    for half in range(2):
        loads.append(pltpu.make_async_copy(slab.at[:, pl.ds(128 * half, 128)], raw.at[half, pl.ds(0, ROWS), :], sems.at[half]))
        loads[-1].start()
    for tile in range(8):
        fill_table(table, FRONT + 128 * tile, angles[:, 128 * tile : 128 * (tile + 1)])
    for load in loads:
        load.wait()
    scalar.wait()
    forward(raw, states, PAD, table, FRONT, flags[0], PAIRS, 128)


def early_kernel(pairing, slab, angles, head_in, far_head_in, states, table, head, far_head, raw, flags, sems):
    @pl.when(lax.axis_index("blk") < EARLY)
    def _():
        evolve(pairing, slab, angles, states, table, raw, flags, sems)


def later_kernel(pairing, slab, angles, states_in, table_in, states, table, raw, flags, sems):
    @pl.when(lax.axis_index("blk") >= EARLY)
    def _():
        evolve(pairing, slab, angles, states, table, raw, flags, sems)


def inner_kernel(
    pairing, offsets, weights, states_in, table, evolved, states, adjoint, gradient, turned, products, out, sems, *scalars
):
    pairing, offsets, weights = fetched((pairing, offsets, weights), scalars)
    lead = pairing[0]

    def weave(i, carry):
        at = pl.multiple_of(i * 128, 128)
        for half in range(2):
            out[half, pl.ds(2 * at + lead + FRONT, 128, stride=2), :] = states[3, 0, half, pl.ds(at + PAD - 1, 128), :]
            out[half, pl.ds(2 * at + lead + FRONT + 1, 128, stride=2), :] = states[3, 1, half, pl.ds(at + PAD, 128), :]
        return carry

    lax.fori_loop(0, PAIRS // 128, weave, 0)
    stores = []
    for half in range(2):
        stores.append(
            pltpu.make_async_copy(out.at[half, pl.ds(FRONT, ROWS), :], evolved.at[:, pl.ds(128 * half, 128)], sems.at[half])
        )
        stores[-1].start()
    blank = jnp.zeros((PAD + 8, 128), jnp.float32)
    for parity in range(2):
        for half in range(2):
            states[LAYERS - 1, parity, half, pl.ds(0, PAD + 8), :] = blank
            states[LAYERS - 1, parity, half, pl.ds(PAD + PAIRS - 8, PAD + 8), :] = blank
    last = states.at[LAYERS - 1]
    band(last, PAD - 8, adjoint, FRONT, offsets, weights, PAIRS + 16, 104, (1, -1), False)
    backward(states, PAD + 256, adjoint, FRONT + 8 + 256, turned, products, table, FRONT + 256, lead, 512, 128)
    for tile in range(4):
        gradient[:, 128 * tile : 128 * (tile + 1)] = summed(products, lead, 128 * tile)
    for store in stores:
        store.wait()


def halo_angles(halo, at, tile):
    return halo[at + 4 * (tile // 2) : at + 4 * (tile // 2) + 4, 128 * (tile % 2) : 128 * (tile % 2) + 128]


def placed(pieces, raw):
    for piece, piece_at, at, rows in pieces:
        for half in range(2):
            raw[half, pl.ds(at, rows), :] = piece[pl.ds(piece_at, rows), 128 * half : 128 * half + 128]


def started(pieces, raw, sems):
    loads = []
    for half in range(2):
        for piece, piece_at, at, rows in pieces:
            load = pltpu.make_async_copy(
                piece.at[pl.ds(piece_at, rows), pl.ds(128 * half, 128)], raw.at[half, pl.ds(at, rows), :], sems.at[len(loads)]
            )
            load.start()
            loads.append(load)
    return loads


def near_tables(side, halo, at, table, halo_table):
    if side == 0:
        fill_table(halo_table, 0, halo_angles(halo, at, 1), 120, 128)
        fill_table(halo_table, 8, halo_angles(halo, at, 2))
        fill_table(halo_table, 136, halo_angles(halo, at, 3))
    else:
        fill_table(halo_table, 16, halo_angles(halo, at, 0))
        fill_table(halo_table, 144, halo_angles(halo, at, 1))
        fill_table(halo_table, 272, halo_angles(halo, at, 2), 0, 16)
    for lane in range(2 * LAYERS):
        if side == 0:
            halo_table[lane, pl.ds(264, 24), :] = table[lane, pl.ds(FRONT, 24), :]
            table[lane, pl.ds(0, FRONT), :] = halo_table[lane, pl.ds(256, 8), :]
        else:
            halo_table[lane, pl.ds(0, 16), :] = table[lane, pl.ds(FRONT + PAIRS - 16, 16), :]
            table[lane, pl.ds(FRONT + PAIRS, 16), :] = halo_table[lane, pl.ds(16, 16), :]


def boundary(side, at, lead, window, states, out, evolved, sems):
    stores = []
    for half in range(2):
        out[half, pl.ds(lead, 16, stride=2), :] = window[3, 0, half, pl.ds(at - 9, 16), :]
        out[half, pl.ds(lead + 1, 16, stride=2), :] = window[3, 1, half, pl.ds(at - 8, 16), :]
        store = pltpu.make_async_copy(
            out.at[half, pl.ds(16, 16), :],
            evolved.at[pl.ds((0, ROWS - 16)[side], 16), pl.ds(128 * half, 128)],
            sems.at[half],
        )
        store.start()
        stores.append(store)
        for parity in range(2):
            for layer in range(LAYERS):
                states[layer, parity, half, pl.ds(PAD + (-8, PAIRS - 8)[side], 16), :] = window[
                    layer, parity, half, pl.ds(at + (-8, 0)[side], 16), :
                ]
    return stores


def left_kernel(
    pairing, offsets, weights, slab, before, evolved_in, states_in, adjoint_in, table_in, inner,
    evolved, states, adjoint, table, halo_table, gradient, raw, window, source, turned, products, out, sems, *scalars,
):
    copies = fetching((pairing, offsets, weights), scalars)
    loads = started(((slab, 0, 8 + NEAR, 40),), raw, sems)
    placed(((before, 0, 8, NEAR),), raw)
    near_tables(0, before, NEAR, table, halo_table)
    for load in loads + copies:
        load.wait()
    pairing, offsets, weights = scalars[:3]
    lead = pairing[0]
    forward(raw, window, FRONT, halo_table, 120, lead, WINDOW, 80)
    stores = boundary(0, FRONT + 144, lead, window, states, out, evolved, sems.at[pl.ds(4, 2)])
    blank = jnp.zeros((272, 128), jnp.float32)
    for half in range(2):
        for parity in range(2):
            source[parity, half, pl.ds(0, 136), :] = blank[:136]
            source[parity, half, pl.ds(136, 144), :] = window[3, parity, half, pl.ds(FRONT + 8, 144), :]
            source[parity, half, pl.ds(280, 272), :] = blank
    band(source, 264, adjoint, FRONT, offsets, weights, 288, 96, (-1,), True)
    band(source, 264, adjoint, FRONT, offsets, weights, 16, 16, (1,), True)
    backward(states, PAD + 120, adjoint, FRONT + 8 + 120, turned, products, table, FRONT + 120, lead, 160, 80)
    lane = lax.broadcasted_iota(jnp.int32, (LAYERS, 128), 1)
    gradient[:, 0:128] = summed(products, lead, 8)
    gradient[:, 128:256] = jnp.where(lane < 16, summed(products, lead, 136), inner[:, 0:128])
    gradient[:, 256:512] = inner[:, 128:384]
    for store in stores:
        store.wait()


def left_far_kernel(
    pairing, offsets, weights, before, before_far, states, table, halo_table, rest, adjoint_in,
    adjoint, gradient, raw, window, source, turned, products, *scalars,
):
    copies = fetching((pairing, offsets, weights), scalars)
    placed(((before_far, SENT - FAR_ROWS, 8, FAR_ROWS), (before, 0, 8 + FAR_ROWS, 32)), raw)
    blank = jnp.zeros((272, 128), jnp.float32)
    for half in range(2):
        for parity in range(2):
            source[parity, half, pl.ds(136, 272), :] = blank
    gradient[:, 128:896] = rest[...]
    for load in copies:
        load.wait()
    pairing, offsets, weights = scalars[:3]
    lead = pairing[0]
    forward(raw, window, FRONT, halo_table, 0, lead, FAR_WINDOW, 136)
    for half in range(2):
        for parity in range(2):
            source[parity, half, pl.ds(8, 128), :] = window[3, parity, half, pl.ds(FRONT, 128), :]
    band(source, 264, adjoint, FRONT, offsets, weights, 144, 144, (-1,), True)
    backward(states, PAD - 8, adjoint, FRONT, turned, products, table, FRONT - 8, lead, 144, 144)
    gradient[:, 0:128] = summed(products, lead, 8)


def right_kernel(
    pairing, offsets, weights, slab, after, inner, left, evolved_in, states_in, adjoint_in, table_in,
    evolved, states, adjoint, table, halo_table, gradient, raw, window, source, turned, products, out, sems, *scalars,
):
    copies = fetching((pairing, offsets, weights), scalars)
    loads = started(((slab, ROWS - 32, 0, 32),), raw, sems)
    placed(((after, 0, 32, HEAD),), raw)
    near_tables(1, after, HEAD, table, halo_table)
    blank = jnp.zeros((272, 128), jnp.float32)
    for half in range(2):
        for parity in range(2):
            source[parity, half, pl.ds(0, 272), :] = blank
            source[parity, half, pl.ds(400, 152), :] = blank[:152]
    gradient[:, 0:512] = left[...]
    for load in loads + copies:
        load.wait()
    pairing, offsets, weights = scalars[:3]
    lead = pairing[0]
    forward(raw, window, FRONT, halo_table, 0, lead, RIGHT_WINDOW, 72)
    stores = boundary(1, FRONT + 8, lead, window, states, out, evolved, sems.at[pl.ds(4, 2)])
    for half in range(2):
        for parity in range(2):
            source[parity, half, pl.ds(272, 128), :] = window[3, parity, half, pl.ds(FRONT + 8, 128), :]
    band(source, 0, adjoint, FRONT + 752, offsets, weights, 288, 144, (1,), True)
    band(source, 272, adjoint, FRONT + PAIRS, offsets, weights, 16, 16, (-1,), True)
    backward(states, PAD + 744, adjoint, FRONT + 8 + 744, turned, products, table, FRONT + 744, lead, 144, 144)
    lane = lax.broadcasted_iota(jnp.int32, (LAYERS, 128), 1)
    gradient[:, 512:640] = jnp.where(lane < 112, inner[:, 384:512], pltpu.roll(summed(products, lead, 8), 112, 1))
    gradient[:, 640:768] = summed(products, lead, 24)
    for store in stores:
        store.wait()


def right_far_kernel(
    pairing, offsets, weights, after, after_far, states, table, halo_table, rest, adjoint_in,
    adjoint, gradient, raw, window, source, turned, products, *scalars,
):
    copies = fetching((pairing, offsets, weights), scalars)
    placed(((after, HEAD - 32, 0, 32), (after_far, 0, 32, HALO - HEAD)), raw)
    blank = jnp.zeros((272, 128), jnp.float32)
    for half in range(2):
        for parity in range(2):
            source[parity, half, pl.ds(0, 272), :] = blank
    gradient[:, 0:768] = rest[:, 0:768]
    for load in copies:
        load.wait()
    pairing, offsets, weights = scalars[:3]
    lead = pairing[0]
    forward(raw, window, FRONT, halo_table, 128, lead, RIGHT_FAR_WINDOW, 152)
    for half in range(2):
        for parity in range(2):
            source[parity, half, pl.ds(272, 144), :] = window[3, parity, half, pl.ds(FRONT + 8, 144), :]
    band(source, 0, adjoint, FRONT + 880, offsets, weights, 160, 160, (1,), True)
    backward(states, PAD + 872, adjoint, FRONT + 8 + 872, turned, products, table, FRONT + 872, lead, 160, 160)
    lane = lax.broadcasted_iota(jnp.int32, (LAYERS, 128), 1)
    gradient[:, 768:896] = jnp.where(lane < 112, rest[:, 768:896], pltpu.roll(summed(products, lead, 8), 112, 1))
    gradient[:, 896:1024] = summed(products, lead, 24)


WHOLE = pl.BlockSpec(memory_space=pltpu.VMEM)
FAR = pl.BlockSpec(memory_space=pl.ANY)

EVOLVED = jax.ShapeDtypeStruct((ROWS, 256), jnp.float32)
STATES = jax.ShapeDtypeStruct((LAYERS, 2, 2, LENGTH, 128), jnp.float32)
ADJOINT = jax.ShapeDtypeStruct((2, 2, PAIRS + 32, 128), jnp.float32)
TABLE = jax.ShapeDtypeStruct((2 * LAYERS, PAIRS + 32, 128), jnp.float32)
HALO_TABLE = jax.ShapeDtypeStruct((2 * LAYERS, 304, 128), jnp.float32)


def limits(flops, traffic, grant=16):
    return dict(
        compiler_params=pltpu.CompilerParams(vmem_limit_bytes=grant * 2**20),
        cost_estimate=pl.CostEstimate(flops=flops, bytes_accessed=traffic, transcendentals=8192),
    )


def room(*shape):
    return pltpu.VMEM(shape, jnp.float32)


def pack_call(slab, angles, pieces, *scalars):
    shapes = [(rows + (0 if lane is None else 8), 256) for _, rows, lane in pieces]

    def kernel(slab, angles, *refs):
        count = len(scalars)
        sources, packed, kept = refs[:count], refs[count : count + len(pieces)], refs[count + len(pieces) : -2]
        tiles, sems = refs[-2], refs[-1]
        copies = [pltpu.make_async_copy(angles, tiles, sems.at[len(pieces)])]
        for n, source in enumerate(sources):
            copies.append(pltpu.make_async_copy(source, kept[n], sems.at[len(pieces) + 1 + n]))
        for n, (first, rows, _) in enumerate(pieces):
            copies.append(
                pltpu.make_async_copy(slab.at[pl.ds(first, rows), :], packed[n].at[pl.ds(0, rows), :], sems.at[n])
            )
        for copy in copies:
            copy.start()
        copies[0].wait()
        for n, (_, rows, lane) in enumerate(pieces):
            if lane is not None:
                for row in range(2):
                    lanes = slice(lane + 256 * row, lane + 256 * (row + 1))
                    packed[n][rows + 4 * row : rows + 4 * (row + 1), :] = tiles[:, lanes]
        for copy in copies[1:]:
            copy.wait()

    return pl.pallas_call(
        kernel,
        out_shape=[jax.ShapeDtypeStruct(shape, jnp.float32) for shape in shapes]
        + [jax.ShapeDtypeStruct(x.shape, x.dtype) for x in (*scalars, angles)],
        in_specs=[pl.BlockSpec(memory_space=pltpu.HBM)] * (2 + len(scalars)),
        out_specs=[WHOLE] * (len(pieces) + len(scalars) + 1),
        scratch_shapes=[pltpu.SemaphoreType.DMA((len(pieces) + len(scalars) + 1,))],
        name="pack",
        **limits(1000, 2**20),
    )(slab, angles, *scalars)


SCALARS = [
    pltpu.SMEM((LAYERS,), jnp.int32),
    pltpu.SMEM((BANDS,), jnp.int32),
    pltpu.SMEM((BANDS,), jnp.float32),
    pltpu.SemaphoreType.DMA((3,)),
]
EVOLVE_ROOM = [room(2, ROWS + 8, 128), pltpu.SMEM((LAYERS,), jnp.int32), pltpu.SemaphoreType.DMA((3,))]


def early_call(pairing, slab, angles, head, far_head):
    return pl.pallas_call(
        early_kernel,
        out_shape=(STATES, TABLE) + tuple(jax.ShapeDtypeStruct(x.shape, x.dtype) for x in (head, far_head)),
        in_specs=[WHOLE, FAR, WHOLE, FAR, FAR],
        out_specs=(WHOLE, WHOLE, FAR, FAR),
        scratch_shapes=EVOLVE_ROOM,
        input_output_aliases={3: 2, 4: 3},
        name="early",
        **limits(12_000_000, 8 * 2**20),
    )(pairing, slab, angles, head, far_head)


def later_call(pairing, slab, angles, states, table):
    return pl.pallas_call(
        later_kernel,
        out_shape=(STATES, TABLE),
        in_specs=[WHOLE, FAR, WHOLE, WHOLE, WHOLE],
        out_specs=(WHOLE, WHOLE),
        scratch_shapes=EVOLVE_ROOM,
        input_output_aliases={3: 0, 4: 1},
        name="later",
        **limits(12_000_000, 8 * 2**20),
    )(pairing, slab, angles, states, table)


def inner_call(pairing, offsets, weights, states, table):
    return pl.pallas_call(
        inner_kernel,
        out_shape=(EVOLVED, STATES, ADJOINT, jax.ShapeDtypeStruct((LAYERS, 512), jnp.float32)),
        in_specs=[WHOLE, WHOLE, WHOLE, WHOLE, WHOLE],
        out_specs=(FAR, WHOLE, WHOLE, WHOLE),
        scratch_shapes=[
            room(LAYERS - 1, 2, 2, 512 + 16, 128),
            room(LAYERS, 512 + 16, 128),
            room(2, ROWS + 16, 128),
            pltpu.SemaphoreType.DMA((2,)),
            *SCALARS,
        ],
        input_output_aliases={3: 1},
        name="inner",
        **limits(50_000_000, 16 * 2**20),
    )(pairing, offsets, weights, states, table)


def left_call(pairing, offsets, weights, slab, before, evolved, states, adjoint, table, inner):
    return pl.pallas_call(
        left_kernel,
        out_shape=(EVOLVED, STATES, ADJOINT, TABLE, HALO_TABLE, jax.ShapeDtypeStruct((LAYERS, 512), jnp.float32)),
        in_specs=[WHOLE, WHOLE, WHOLE, FAR, WHOLE, FAR, WHOLE, WHOLE, WHOLE, WHOLE],
        out_specs=(FAR, WHOLE, WHOLE, WHOLE, WHOLE, WHOLE),
        scratch_shapes=[
            room(2, 328, 128),
            room(LAYERS, 2, 2, WINDOW + 16, 128),
            room(2, 2, 552, 128),
            room(LAYERS - 1, 2, 2, 160 + 16, 128),
            room(LAYERS, 280, 128),
            room(2, 40, 128),
            pltpu.SemaphoreType.DMA((6,)),
            *SCALARS,
        ],
        input_output_aliases={5: 0, 6: 1, 7: 2, 8: 3},
        name="left",
        **limits(15_000_000, 8 * 2**20),
    )(pairing, offsets, weights, slab, before, evolved, states, adjoint, table, inner)


def left_far_call(pairing, offsets, weights, before, before_far, states, table, halo_table, rest, adjoint):
    return pl.pallas_call(
        left_far_kernel,
        out_shape=(ADJOINT, jax.ShapeDtypeStruct((LAYERS, 896), jnp.float32)),
        in_specs=[WHOLE, WHOLE, WHOLE] + [WHOLE] * 7,
        out_specs=(WHOLE, WHOLE),
        scratch_shapes=[
            room(2, 280, 128),
            room(LAYERS, 2, 2, FAR_WINDOW + 16, 128),
            room(2, 2, 408, 128),
            room(LAYERS - 1, 2, 2, 144 + 16, 128),
            room(LAYERS, 160, 128),
            *SCALARS,
        ],
        input_output_aliases={9: 0},
        name="left_far",
        **limits(10_000_000, 8 * 2**20),
    )(pairing, offsets, weights, before, before_far, states, table, halo_table, rest, adjoint)


def right_call(*operands):
    return pl.pallas_call(
        right_kernel,
        out_shape=(EVOLVED, STATES, ADJOINT, TABLE, HALO_TABLE, jax.ShapeDtypeStruct((LAYERS, 768), jnp.float32)),
        in_specs=[WHOLE, WHOLE, WHOLE, FAR] + [WHOLE] * 3 + [FAR, WHOLE, WHOLE, WHOLE],
        out_specs=(FAR, WHOLE, WHOLE, WHOLE, WHOLE, WHOLE),
        scratch_shapes=[
            room(2, 2 * RIGHT_WINDOW + 8, 128),
            room(LAYERS, 2, 2, RIGHT_WINDOW + 16, 128),
            room(2, 2, 560, 128),
            room(LAYERS - 1, 2, 2, 144 + 16, 128),
            room(LAYERS, 168, 128),
            room(2, 40, 128),
            pltpu.SemaphoreType.DMA((6,)),
            *SCALARS,
        ],
        input_output_aliases={7: 0, 8: 1, 9: 2, 10: 3},
        name="right",
        **limits(15_000_000, 8 * 2**20),
    )(*operands)


def right_far_call(*operands):
    return pl.pallas_call(
        right_far_kernel,
        out_shape=(ADJOINT, jax.ShapeDtypeStruct((LAYERS, PAIRS), jnp.float32)),
        in_specs=[WHOLE, WHOLE, WHOLE] + [WHOLE] * 7,
        out_specs=(WHOLE, WHOLE),
        scratch_shapes=[
            room(2, 2 * RIGHT_FAR_WINDOW + 8, 128),
            room(LAYERS, 2, 2, RIGHT_FAR_WINDOW + 16, 128),
            room(2, 2, 440, 128),
            room(LAYERS - 1, 2, 2, 160 + 16, 128),
            room(LAYERS, 176, 128),
            *SCALARS,
        ],
        input_output_aliases={9: 0},
        name="right_far",
        **limits(10_000_000, 8 * 2**20),
    )(*operands)


def on_device(slab, angles, pairing, band_offsets, band_weights):
    slab = pltpu.with_memory_space_constraint(slab, pltpu.HBM)
    angles = pltpu.with_memory_space_constraint(angles, pltpu.HBM)
    count = lax.axis_size("blk")
    onward = [(i, (i + 1) % count) for i in range(count)]
    back = [((i + 1) % count, i) for i in range(count)]
    scalars = [pltpu.with_memory_space_constraint(x, pltpu.HBM) for x in (pairing, band_offsets, band_weights)]
    tail, far_tail, head, far_head, *scalars, angles_near = pack_call(
        slab, angles, ((ROWS - NEAR, NEAR, 512), (ROWS - NEAR - SENT, SENT, None), (0, HEAD, 0), (HEAD, HALO - HEAD, None)),
        *scalars,
    )
    before = lax.ppermute(tail, "blk", onward)
    before_far = lax.ppermute(far_tail, "blk", onward)
    states, table, head, far_head = early_call(scalars[0], slab, angles_near, head, far_head)
    after = lax.ppermute(head, "blk", back)
    after_far = lax.ppermute(far_head, "blk", back)
    states, table = later_call(scalars[0], slab, angles_near, states, table)
    evolved, states, adjoint, inner = inner_call(*scalars, states, table)
    evolved, states, adjoint, table, left_table, left = left_call(
        *scalars, slab, before, evolved, states, adjoint, table, inner
    )
    evolved, states, adjoint, table, right_table, rest = right_call(
        *scalars, slab, after, inner, left, evolved, states, adjoint, table
    )
    adjoint, rest = left_far_call(*scalars, before, before_far, states, table, left_table, rest, adjoint)
    _, gradient = right_far_call(*scalars, after, after_far, states, table, right_table, rest, adjoint)
    columns = lax.axis_size("col")
    step = columns // 2
    while step:
        gradient = gradient + lax.ppermute(gradient, "col", [(i, i ^ step) for i in range(columns)])
        step //= 2
    return (evolved, gradient)


def solution(mesh):
    in_specs = (P("blk", "col"), P(None, "blk"), P(), P(), P())
    out_specs = (P("blk", "col"), P(None, "blk"))
    return jax.shard_map(
        on_device, mesh=mesh, in_specs=in_specs, out_specs=out_specs, check_vma=False
    )
```
